256 devices in a mesh: tm: 128 (over z, x_lo, y, core), head: 2 (over x_hi).
Axes of the slice: x: 4 (x_hi: 2, x_lo: 2; x = x_hi * 2 + x_lo), y: 4, z: 8, core: 2. Of those that a mesh axis runs over, the one named last changes fastest.
Arguments:
- inputs: bfloat16 [32768, 1024], P('tm', 'head'), may hold values from -8 to 8
- w_query: bfloat16 [1024, 1024], P(None, 'head'), may hold values from -1 to 1
- w_key: bfloat16 [1024, 1024], P(None, 'head'), may hold values from -1 to 1
- w_value: bfloat16 [1024, 1024], P(None, 'head'), may hold values from -0.1875 to 0.1875
- w_out: bfloat16 [1024, 1024], P('head'), may hold values from -0.1875 to 0.1875
- kernel: float32 [9, 1024], P(None, 'head'), may hold values from -1.2 to 1.6
- cotangent: bfloat16 [32768, 1024], P('tm', 'head'), may hold values from -9 to 9
Outputs:
- output: bfloat16 [32768, 1024], P('tm', 'head')
- grad_inputs: bfloat16 [32768, 1024], P('tm', 'head')
- grad_kernel: float32 [9, 1024], P(None, 'head')
The draws below stay inside these ranges and needn't reach their ends.
All inputs are finite; a program needn't handle non-finite values.
Results may differ from the reference program's by a relative error of at most 0.008.
Values may be sent and summed in bfloat16 or wider, within the bound.
No kernel may reach another device: no remote copies, remote signals or barrier semaphores. Data moves between devices by JAX's collectives and lax.ppermute only.
A program may use at most 64 MiB of HBM per device.

```python
import math
import jax
import jax.numpy as jnp
from jax import lax

D = 1024
HEADS = 8
HEAD_DIM = 128
BLOCK = 128
CONTEXT = 2
KW = 9
SEQ = 32768


def feature_ramp(low):
    return low + jnp.arange(D, dtype=jnp.float32) / (D - 1)


def draw_inputs(key, part):
    own = jax.random.fold_in(key, 7)
    noise_key = jax.random.fold_in(own, 0)
    noise = jnp.clip(jax.random.normal(noise_key, (SEQ, D), jnp.float32), -6.0, 6.0)
    return noise.astype(jnp.bfloat16)


def draw_w_query(key, part):
    own = jax.random.fold_in(key, 11)
    weights = jnp.clip(jax.random.normal(own, (D, D), jnp.float32), -6.0, 6.0) / math.sqrt(D)
    return weights.astype(jnp.bfloat16)


def draw_w_key(key, part):
    own = jax.random.fold_in(key, 13)
    weights = jnp.clip(jax.random.normal(own, (D, D), jnp.float32), -6.0, 6.0) / math.sqrt(D)
    return weights.astype(jnp.bfloat16)


def draw_kernel(key, part):
    own = jax.random.fold_in(key, 17)
    taps = jnp.clip(jax.random.normal(own, (KW, D), jnp.float32), -4.0, 4.0) / 3.0
    return (taps + 0.25).astype(jnp.float32)


def draw_cotangent(key, part):
    own = jax.random.fold_in(key, 19)
    noise_key, frame_key = jax.random.split(own)
    noise = jnp.clip(jax.random.normal(noise_key, (SEQ, D), jnp.float32), -4.0, 4.0)
    frames = jnp.clip(jax.random.normal(frame_key, (SEQ, 1), jnp.float32), -3.0, 3.0)
    ramp = feature_ramp(0.5)
    return (noise + frames * ramp[None, :]).astype(jnp.bfloat16)


def block_scale(own_key, dims, pieces, smallest, largest):
    def one(axis_at, parts):
        steps = jax.random.uniform(jax.random.fold_in(jax.random.fold_in(own_key, 6), axis_at), (parts,), jnp.float32, smallest / len(pieces), largest / len(pieces))
        return jnp.repeat(jnp.exp(steps), dims[axis_at] // parts).reshape((-1,) + (1,) * (len(dims) - axis_at - 1))

    loudness = one(*pieces[0])
    for cut in pieces[1:]:
        loudness = loudness * one(*cut)
    return loudness


def centred(stream_key, extent, width, limit, pieces=(), held_as=jnp.bfloat16):
    drawn = width * jax.random.normal(stream_key, extent, jnp.float32)
    if pieces:
        drawn = drawn * block_scale(stream_key, extent, pieces, -0.22, 0.18)
    return jnp.clip(drawn, -limit, limit).astype(held_as)


def setup_inputs(seed: int = 0) -> dict:
    key_of = jax.random.split(jax.random.key(seed), 8)
    inputs = draw_inputs(jax.random.fold_in(key_of[7], 71), 0)
    w_query = draw_w_query(jax.random.fold_in(key_of[7], 71), 0)
    w_key = draw_w_key(jax.random.fold_in(key_of[7], 71), 0)
    w_value = centred(key_of[3], (D, D), D ** -0.5, 0.1875, ((1, 2),))
    w_out = centred(key_of[4], (D, D), D ** -0.5, 0.1875, ((0, 2),))
    kernel = draw_kernel(jax.random.fold_in(key_of[7], 71), 0)
    cotangent = draw_cotangent(jax.random.fold_in(key_of[7], 71), 0)
    return dict(inputs=inputs, w_query=w_query, w_key=w_key, w_value=w_value, w_out=w_out, kernel=kernel, cotangent=cotangent)


EPSILON = 1e-05
MASKED = -1e+30

def settle(values):
    return lax.optimization_barrier(values.astype(jnp.bfloat16)).astype(jnp.float32)

def normalize(values):
    center = lax.optimization_barrier(jnp.mean(values, axis=1))
    spread = lax.optimization_barrier(jnp.mean(values * values, axis=1)) - center * center
    rstd = lax.rsqrt(spread + EPSILON)
    return ((values - center[:, None]) * rstd[:, None], rstd)

def reference(inputs, w_query, w_key, w_value, w_out, kernel, cotangent):
    total = inputs.shape[0]
    blocks = total // BLOCK
    margin = CONTEXT * BLOCK
    span = (2 * CONTEXT + 1) * BLOCK
    scale = HEAD_DIM ** (-0.5)
    half = KW // 2
    start_f = inputs.astype(jnp.float32)
    normed, rstd_one = normalize(start_f)
    normed_b = normed.astype(jnp.bfloat16)
    query = jnp.dot(normed_b, w_query, preferred_element_type=jnp.float32).astype(jnp.bfloat16)
    keys = jnp.dot(normed_b, w_key, preferred_element_type=jnp.float32).astype(jnp.bfloat16)
    values = jnp.dot(normed_b, w_value, preferred_element_type=jnp.float32).astype(jnp.bfloat16)
    keys_pad = jnp.pad(keys, ((margin, margin), (0, 0)))
    values_pad = jnp.pad(values, ((margin, margin), (0, 0)))
    positions = jnp.arange(total + 2 * margin, dtype=jnp.int32) - margin
    valid_all = (positions >= 0) & (positions < total)

    def block_probs(index):
        first = index * BLOCK
        q_blk = lax.dynamic_slice_in_dim(query, first, BLOCK, 0).astype(jnp.float32).reshape(BLOCK, HEADS, HEAD_DIM)
        k_win = lax.dynamic_slice_in_dim(keys_pad, first, span, 0).astype(jnp.float32).reshape(span, HEADS, HEAD_DIM)
        v_win = lax.dynamic_slice_in_dim(values_pad, first, span, 0).astype(jnp.float32).reshape(span, HEADS, HEAD_DIM)
        valid = lax.dynamic_slice_in_dim(valid_all, first, span, 0)
        scores = jnp.einsum('qhe,khe->hqk', q_blk, k_win) * scale
        scores = jnp.where(valid[None, None, :], scores, MASKED)
        top = lax.optimization_barrier(jnp.max(scores, axis=-1, keepdims=True))
        logsum = top + jnp.log(lax.optimization_barrier(jnp.sum(jnp.exp(scores - top), axis=-1, keepdims=True)))
        probs = jnp.exp(scores - logsum)
        return (q_blk, k_win, v_win, probs)

    def forward_block(index):
        q_blk, k_win, v_win, probs = block_probs(index)
        return jnp.einsum('hqk,khe->qhe', settle(probs), v_win).reshape(BLOCK, D)
    block_ids = jnp.arange(blocks, dtype=jnp.int32)
    attended = lax.map(forward_block, block_ids).reshape(total, D).astype(jnp.bfloat16)
    hidden = start_f + jnp.dot(attended, w_out, preferred_element_type=jnp.float32)
    normed_two, rstd_two = normalize(hidden)
    conv_pad = jnp.pad(normed_two, ((half, half), (0, 0)))
    mixed = jnp.zeros_like(hidden)
    for tap in range(KW):
        mixed = mixed + kernel[tap][None, :] * conv_pad[tap:tap + total]
    gate = jax.nn.sigmoid(mixed)
    output = (hidden + mixed * gate).astype(jnp.bfloat16)
    upstream = cotangent.astype(jnp.float32)
    grad_mixed = upstream * gate * (1.0 + mixed * (1.0 - gate))
    grad_pad = jnp.pad(grad_mixed, ((half, half), (0, 0)))
    grad_normed = jnp.zeros_like(hidden)
    for tap in range(KW):
        grad_normed = grad_normed + kernel[tap][None, :] * grad_pad[2 * half - tap:2 * half - tap + total]
    grad_kernel = jnp.stack([lax.optimization_barrier(jnp.sum(grad_mixed * conv_pad[tap:tap + total], axis=0)) for tap in range(KW)])
    grad_hidden = upstream + rstd_two[:, None] * (grad_normed - lax.optimization_barrier(jnp.mean(grad_normed, axis=1, keepdims=True)) - normed_two * lax.optimization_barrier(jnp.mean(grad_normed * normed_two, axis=1, keepdims=True)))
    grad_att = jnp.dot(grad_hidden.astype(jnp.bfloat16), w_out.T, preferred_element_type=jnp.float32).astype(jnp.bfloat16)

    def backward_block(carry, index):
        q_blk, k_win, v_win, probs = block_probs(index)
        g_blk = lax.dynamic_slice_in_dim(grad_att, index * BLOCK, BLOCK, 0).astype(jnp.float32).reshape(BLOCK, HEADS, HEAD_DIM)
        dots = jnp.einsum('qhe,khe->hqk', g_blk, v_win)
        delta = lax.optimization_barrier(jnp.sum(probs * dots, axis=-1, keepdims=True))
        dscore = settle(probs * (dots - delta) * scale)
        grad_q = jnp.einsum('hqk,khe->qhe', dscore, k_win).reshape(BLOCK, D)
        grad_k = jnp.einsum('hqk,qhe->khe', dscore, q_blk).reshape(span, D)
        grad_v = jnp.einsum('hqk,qhe->khe', settle(probs), g_blk).reshape(span, D)
        current = lax.dynamic_slice_in_dim(carry, index * BLOCK, span, 1)
        carry = lax.dynamic_update_slice_in_dim(carry, current + jnp.stack((grad_k, grad_v)), index * BLOCK, 1)
        return (carry, grad_q)
    empty = jnp.zeros((2, total + 2 * margin, D), jnp.float32)
    folded, grad_q_all = lax.scan(backward_block, empty, block_ids)
    grad_query = grad_q_all.reshape(total, D).astype(jnp.bfloat16)
    grad_key = folded[0, margin:margin + total].astype(jnp.bfloat16)
    grad_value = folded[1, margin:margin + total].astype(jnp.bfloat16)
    grad_n1 = jnp.dot(grad_query, w_query.T, preferred_element_type=jnp.float32)
    grad_n1 = grad_n1 + jnp.dot(grad_key, w_key.T, preferred_element_type=jnp.float32)
    grad_n1 = grad_n1 + jnp.dot(grad_value, w_value.T, preferred_element_type=jnp.float32)
    grad_inputs = grad_hidden + rstd_one[:, None] * (grad_n1 - lax.optimization_barrier(jnp.mean(grad_n1, axis=1, keepdims=True)) - normed * lax.optimization_barrier(jnp.mean(grad_n1 * normed, axis=1, keepdims=True)))
    return (output, grad_inputs.astype(jnp.bfloat16), grad_kernel)
```

```python
import functools
import jax
import jax.numpy as jnp
from jax import lax
from jax.experimental import pallas as pl
from jax.experimental.pallas import tpu as pltpu
from jax.sharding import PartitionSpec as P

D = 1024
HEAD_DIM = 128
BLOCK = 128
CONTEXT = 2
KW = 9
EPSILON = 1e-05
MASKED = -1e30

ROWS = CONTEXT * BLOCK
SHARE = 512
HEADS = SHARE // HEAD_DIM
LANES = 128
EDGE = 16
PACK = ROWS + 2 * EDGE
CHUNKS = D // LANES
HALF_CHUNKS = SHARE // LANES
PAD = 16
EXT = ROWS + 2 * PAD
HALF = KW // 2
SCALE = HEAD_DIM ** (-0.5)
F32 = jnp.float32
BF16 = jnp.bfloat16


def nn(a, b):
    return lax.dot_general(a, b, (((1,), (0,)), ((), ())), preferred_element_type=F32)


def nt(a, b):
    return lax.dot_general(a, b, (((1,), (1,)), ((), ())), preferred_element_type=F32)


def tn(a, b):
    return lax.dot_general(a, b, (((0,), (0,)), ((), ())), preferred_element_type=F32)


def row_sum(a):
    return jnp.sum(a, axis=1, keepdims=True)


def moments(a, b):
    center = (row_sum(a) + row_sum(b)) * (1.0 / D)
    spread = (row_sum(a * a) + row_sum(b * b)) * (1.0 / D) - center * center
    return center, lax.rsqrt(spread + EPSILON)


def norm_pair(a, b):
    a = a.astype(F32)
    b = b.astype(F32)
    center, rstd = moments(a, b)
    return (a - center) * rstd, (b - center) * rstd, rstd


def own_other(h):
    own = pl.ds(pl.multiple_of(h * SHARE, SHARE), SHARE)
    other = pl.ds(pl.multiple_of((1 - h) * SHARE, SHARE), SHARE)
    return own, other


def lanes_of(head):
    return slice(head * HEAD_DIM, (head + 1) * HEAD_DIM)


def band_bias(right, valid):
    row = (lax.broadcasted_iota(jnp.int32, (ROWS, ROWS), 0) >= BLOCK).astype(jnp.int32)
    col = (lax.broadcasted_iota(jnp.int32, (ROWS, ROWS), 1) >= BLOCK).astype(jnp.int32)
    hidden = ((row - col) == 1 - 2 * right) | (valid == 0)
    return jnp.where(hidden, MASKED, 0.0).astype(F32)


def own_kernel(info, xo, mp, wq, wk, wv, q, k, v):
    own, other = own_other(info[0])
    no, np_, _ = norm_pair(xo[...], mp[:ROWS, :])
    no = no.astype(BF16)
    np_ = np_.astype(BF16)
    for w, out in ((wq, q), (wk, k), (wv, v)):
        out[...] = (nn(no, w[own, :]) + nn(np_, w[other, :])).astype(BF16)


def halo_kv(info, mo, mp, wk, wv, k, v):
    own, other = own_other(info[0])
    no, np_, _ = norm_pair(mo[:ROWS, :], mp[:ROWS, :])
    no = no.astype(BF16)
    np_ = np_.astype(BF16)
    for w, out in ((wk, k), (wv, v)):
        out[...] = (nn(no, w[own, :]) + nn(np_, w[other, :])).astype(BF16)


def first_kernel(info, mo, mp, wk, wv, q, k, v, ka, va, e, acc, top, total):
    halo_kv(info, mo, mp, wk, wv, ka, va)
    bias = band_bias(1 - info[1], 1)
    for head in range(HEADS):
        f = lanes_of(head)
        qh = q[:, f]
        s_own = nt(qh, k[:, f]) * SCALE
        s_a = nt(qh, ka[:, f]) * SCALE + bias
        m = jnp.maximum(jnp.max(s_own, axis=1, keepdims=True), jnp.max(s_a, axis=1, keepdims=True))
        e_own = jnp.exp(s_own - m)
        e_a = jnp.exp(s_a - m)
        total[head] = jnp.broadcast_to(row_sum(e_own) + row_sum(e_a), (ROWS, LANES))
        top[head] = jnp.broadcast_to(m, (ROWS, LANES))
        e_own = e_own.astype(BF16)
        e_a = e_a.astype(BF16)
        e[head, :, :ROWS] = e_own
        e[head, :, ROWS:] = e_a
        acc[:, f] = nn(e_own, v[:, f]) + nn(e_a, va[:, f])


def second_kernel(
    info, mo, mp, wk, wv, wo, q, acc, top, total, kb, vb, e, weight, att, part, edge_a, edge_b
):
    halo_kv(info, mo, mp, wk, wv, kb, vb)
    bias = band_bias(info[1], info[2])
    for head in range(HEADS):
        f = lanes_of(head)
        s = nt(q[:, f], kb[:, f]) * SCALE + bias
        m1 = top[head][:, :1]
        m = jnp.maximum(m1, jnp.max(s, axis=1, keepdims=True))
        shrink = jnp.exp(m1 - m)
        eb = jnp.exp(s - m)
        inverse = 1.0 / (total[head][:, :1] * shrink + row_sum(eb))
        eb = eb.astype(BF16)
        e[head] = eb
        o = (acc[:, f] * shrink + nn(eb, vb[:, f])) * inverse
        att[:, f] = o.astype(BF16)
        weight[0, head] = jnp.broadcast_to(shrink * inverse, (ROWS, LANES))
        weight[1, head] = jnp.broadcast_to(inverse, (ROWS, LANES))
    own, other = own_other(info[0])
    part[:, :SHARE] = nn(att[...], wo[:, own]).astype(BF16)
    part[:, SHARE:] = nn(att[...], wo[:, other]).astype(BF16)
    odd = info[1]
    last = ROWS - EDGE
    edge_a[...] = part[pl.ds(pl.multiple_of((1 - odd) * last, EDGE), EDGE), :]
    edge_b[...] = part[pl.ds(pl.multiple_of(odd * last, EDGE), EDGE), :]


def conv_kernel(
    info, xo, mp, a0, a1, b0, b1, part, part_p, ea, eb, e2, co, cp, to, tp, wo,
    output, dh, datt, gk,
    n2s, cs, dzs, dns, hs, taps, rs2, sum0, sum1, dhb,
):
    odd = info[1]
    own, other = own_other(info[0])
    is_odd = odd == 1
    step = 32
    for c in range(HALF_CHUNKS):
        f = slice(c * LANES, (c + 1) * LANES)
        taps[c, :KW, :] = to[:, f]
        taps[HALF_CHUNKS + c, :KW, :] = tp[:, f]

    def rows_in(index, carry):
        r = pl.multiple_of(index * step, step)
        rows = pl.ds(r, step)
        held = pl.ds(pl.multiple_of(PAD + r, PAD), step)
        p = part[rows, :].astype(F32)
        pp = part_p[rows, :].astype(F32)
        ho = xo[rows, :].astype(F32) + p[:, :SHARE] + pp[:, SHARE:]
        hp = mp[rows, :].astype(F32) + p[:, SHARE:] + pp[:, :SHARE]
        center, rstd = moments(ho, hp)
        hs[rows, :] = ho
        rs2[rows, :] = jnp.broadcast_to(rstd, (step, LANES))
        ctan = co[rows, :].astype(F32)
        ctan_p = cp[rows, :].astype(F32)
        for c in range(HALF_CHUNKS):
            f = slice(c * LANES, (c + 1) * LANES)
            n2s[c, held, :] = (ho[:, f] - center) * rstd
            n2s[HALF_CHUNKS + c, held, :] = (hp[:, f] - center) * rstd
            cs[c, held, :] = ctan[:, f]
            cs[HALF_CHUNKS + c, held, :] = ctan_p[:, f]
        return carry

    lax.fori_loop(0, ROWS // step, rows_in, 0)

    pa = ea[...].astype(F32)
    pb = eb[...].astype(F32)
    qb = e2[:EDGE, :].astype(F32)
    qa = e2[EDGE:, :].astype(F32)
    sides = (
        (slice(ROWS - EDGE, ROWS), slice(ROWS + EDGE, PACK), is_odd, 0, info[3]),
        (slice(0, EDGE), slice(ROWS, ROWS + EDGE), jnp.logical_not(is_odd), PAD + ROWS, info[4]),
    )
    for x_rows, c_rows, from_a, at, valid in sides:
        def pick(one, two):
            return jnp.where(from_a, one.astype(F32), two.astype(F32))

        pe = pick(pa, pb)
        pe_p = pick(qa, qb)
        ho = pick(a0[x_rows, :], b0[x_rows, :]) + pe[:, :SHARE] + pe_p[:, SHARE:]
        hp = pick(a1[x_rows, :], b1[x_rows, :]) + pe[:, SHARE:] + pe_p[:, :SHARE]
        center, rstd = moments(ho, hp)
        ctan = pick(a0[c_rows, :], b0[c_rows, :])
        ctan_p = pick(a1[c_rows, :], b1[c_rows, :])
        inside = valid == 1
        for c in range(HALF_CHUNKS):
            f = slice(c * LANES, (c + 1) * LANES)
            for d, hh, cc in ((c, ho, ctan), (HALF_CHUNKS + c, hp, ctan_p)):
                n2s[d, at:at + EDGE, :] = jnp.where(inside, (hh[:, f] - center) * rstd, 0.0)
                cs[d, at:at + EDGE, :] = jnp.where(inside, cc[:, f], 0.0)

    piece = 136

    def forward(c, carry, mine):
        w = taps[c]
        for r0 in (8, 8 + piece):
            z = w[0:1, :] * n2s[c, r0 - HALF:r0 - HALF + piece, :]
            for tap in range(1, KW):
                at = r0 + tap - HALF
                z = z + w[tap:tap + 1, :] * n2s[c, at:at + piece, :]
            gate = jax.nn.sigmoid(z)
            dzs[c, r0:r0 + piece, :] = cs[c, r0:r0 + piece, :] * gate * (1.0 + z * (1.0 - gate))
            if mine:
                lo = max(r0, PAD)
                hi = min(r0 + piece, PAD + ROWS)
                lane = pl.ds(pl.multiple_of(c * LANES, LANES), LANES)
                mix = (z * gate)[lo - r0:hi - r0, :]
                hs[lo - PAD:hi - PAD, lane] = hs[lo - PAD:hi - PAD, lane] + mix
        if mine:
            lane = pl.ds(pl.multiple_of(c * LANES, LANES), LANES)
            dz = dzs[c, PAD:PAD + ROWS, :]
            for tap in range(KW):
                at = PAD + tap - HALF
                gk[tap:tap + 1, lane] = jnp.sum(
                    dz * n2s[c, at:at + ROWS, :], axis=0, keepdims=True
                )
        return carry

    lax.fori_loop(0, HALF_CHUNKS, functools.partial(forward, mine=True), 0)
    lax.fori_loop(HALF_CHUNKS, CHUNKS, functools.partial(forward, mine=False), 0)
    output[...] = hs[...].astype(BF16)

    sum0[...] = jnp.zeros_like(sum0)
    sum1[...] = jnp.zeros_like(sum1)

    def backward(c, carry):
        w = taps[c]
        for r0 in (0, ROWS // 2):
            at = PAD + r0 + HALF
            g = w[0:1, :] * dzs[c, at:at + ROWS // 2, :]
            for tap in range(1, KW):
                at = PAD + r0 + HALF - tap
                g = g + w[tap:tap + 1, :] * dzs[c, at:at + ROWS // 2, :]
            dns[c, r0:r0 + ROWS // 2, :] = g
            half = slice(r0, r0 + ROWS // 2)
            sum0[half, :] = sum0[half, :] + g
            sum1[half, :] = sum1[half, :] + g * n2s[c, PAD + r0:PAD + r0 + ROWS // 2, :]
        return carry

    lax.fori_loop(0, CHUNKS, backward, 0)
    sum0[...] = jnp.broadcast_to(row_sum(sum0[...]) * (1.0 / D), (ROWS, LANES))
    sum1[...] = jnp.broadcast_to(row_sum(sum1[...]) * (1.0 / D), (ROWS, LANES))

    def finish(c, carry, mine):
        lane = pl.ds(pl.multiple_of(c * LANES, LANES), LANES)
        value = cs[c, PAD:PAD + ROWS, :] + rs2[...] * (
            dns[c] - sum0[...] - n2s[c, PAD:PAD + ROWS, :] * sum1[...]
        )
        if mine:
            dh[:, lane] = value
        dhb[:, lane] = value.astype(BF16)
        return carry

    lax.fori_loop(0, HALF_CHUNKS, functools.partial(finish, mine=True), 0)
    lax.fori_loop(HALF_CHUNKS, CHUNKS, functools.partial(finish, mine=False), 0)
    datt[...] = (nt(dhb[:, :SHARE], wo[:, own]) + nt(dhb[:, SHARE:], wo[:, other])).astype(BF16)


def pair_grad(qh, kh, vh, gh, eh, wh, delta):
    dots = nt(gh, vh)
    p = eh.astype(F32) * wh
    ds = (p * (dots - delta) * SCALE).astype(BF16)
    return nn(ds, kh), tn(ds, qh), tn(p.astype(BF16), gh)


def back_b_kernel(q, kb, vb, datt, att, e, weight, dq, dkv):
    for head in range(HEADS):
        f = lanes_of(head)
        gh = datt[:, f]
        delta = row_sum(gh.astype(F32) * att[:, f].astype(F32))
        d_q, d_k, d_v = pair_grad(
            q[:, f], kb[:, f], vb[:, f], gh, e[head], weight[1, head][:, :1], delta
        )
        dq[:, f] = d_q
        dkv[0, :, f] = d_k.astype(BF16)
        dkv[1, :, f] = d_v.astype(BF16)


def back_own_kernel(info, q, k, v, ka, va, datt, att, e, weight, dq_b, wq, dkv_a, dkv, pin):
    dq = []
    for head in range(HEADS):
        f = lanes_of(head)
        gh = datt[:, f]
        delta = row_sum(gh.astype(F32) * att[:, f].astype(F32))
        wh = weight[0, head][:, :1]
        q_a, k_a, v_a = pair_grad(q[:, f], ka[:, f], va[:, f], gh, e[head, :, ROWS:], wh, delta)
        dkv_a[0, :, f] = k_a.astype(BF16)
        dkv_a[1, :, f] = v_a.astype(BF16)
        q_o, k_o, v_o = pair_grad(q[:, f], k[:, f], v[:, f], gh, e[head, :, :ROWS], wh, delta)
        dkv[0, :, f] = k_o
        dkv[1, :, f] = v_o
        dq.append((dq_b[:, f] + q_a + q_o).astype(BF16))
    own, other = own_other(info[0])
    dq = jnp.concatenate(dq, axis=1)
    pin[:, :SHARE] = nt(dq, wq[own, :])
    pin[:, SHARE:] = nt(dq, wq[other, :])


def project_kernel(info, xo, mp, dkv, got_a, got_b, pin, wk, wv, send, keep, stat):
    own, other = own_other(info[0])
    dk = (dkv[0] + got_a[0].astype(F32) + got_b[0].astype(F32)).astype(BF16)
    dv = (dkv[1] + got_a[1].astype(F32) + got_b[1].astype(F32)).astype(BF16)
    p_own = pin[:, :SHARE] + nt(dk, wk[own, :]) + nt(dv, wv[own, :])
    p_other = pin[:, SHARE:] + nt(dk, wk[other, :]) + nt(dv, wv[other, :])
    no, np_, _ = norm_pair(xo[...], mp[:ROWS, :])
    s0 = row_sum(p_own) + row_sum(p_other)
    s1 = row_sum(p_own * no) + row_sum(p_other * np_)
    keep[...] = p_own
    send[:, :SHARE] = p_other.astype(BF16)
    lane = lax.broadcasted_iota(jnp.int32, (ROWS, LANES), 1)
    s0_hi = s0.astype(BF16).astype(F32)
    s1_hi = s1.astype(BF16).astype(F32)
    packed = jnp.where(lane == 0, s0_hi, 0.0)
    packed = jnp.where(lane == 1, s0 - s0_hi, packed)
    packed = jnp.where(lane == 2, s1_hi, packed)
    packed = jnp.where(lane == 3, s1 - s1_hi, packed)
    send[:, SHARE:] = packed.astype(BF16)
    stat[...] = jnp.where(lane == 0, s0, jnp.where(lane == 2, s1, 0.0))


def final_kernel(xo, mp, keep, stat, got, dh, grad):
    no, _, rstd = norm_pair(xo[...], mp[:ROWS, :])
    dn1 = keep[...] + got[:, :SHARE].astype(F32)
    lane = lax.broadcasted_iota(jnp.int32, (ROWS, LANES), 1)
    sums = stat[...] + got[:, SHARE:].astype(F32)
    s0 = row_sum(jnp.where(lane < 2, sums, 0.0)) * (1.0 / D)
    s1 = row_sum(jnp.where(lane < 2, 0.0, sums)) * (1.0 / D)
    grad[...] = (dh[...] + rstd * (dn1 - s0 - no * s1)).astype(BF16)


def call(kernel, args, outs, scratch=(), smem=True, us=1.0):
    whole = pl.BlockSpec(memory_space=pltpu.VMEM)
    specs = [whole] * len(args)
    if smem:
        specs[0] = pl.BlockSpec(memory_space=pltpu.SMEM)
    return pl.pallas_call(
        kernel,
        out_shape=[jax.ShapeDtypeStruct(shape, dtype) for shape, dtype in outs],
        in_specs=specs,
        out_specs=[whole] * len(outs),
        scratch_shapes=[pltpu.VMEM(shape, dtype) for shape, dtype in scratch],
        compiler_params=pltpu.CompilerParams(vmem_limit_bytes=40 * 1024 * 1024),
        cost_estimate=pl.CostEstimate(
            flops=int(us * 1e9), bytes_accessed=int(us * 1e6), transcendentals=0
        ),
    )(*args)


def local(inputs, w_query, w_key, w_value, w_out, kernel, cotangent):
    count = lax.axis_size("tm")
    assert inputs.shape == (ROWS, SHARE) and count % 2 == 0
    place = lax.axis_index("tm")
    odd = place % 2
    not_first = (place > 0).astype(jnp.int32)
    not_last = (place < count - 1).astype(jnp.int32)
    info = jnp.stack(
        [lax.axis_index("head"), odd, jnp.where(odd == 1, not_last, not_first), not_first, not_last]
    ).astype(jnp.int32)

    def over_head(value):
        return lax.ppermute(value, "head", [(0, 1), (1, 0)])

    def over_a(value):
        return lax.ppermute(value, "tm", [(i, i ^ 1) for i in range(count)])

    def over_b(value):
        pairs = [(i, i + 1) for i in range(1, count - 1, 2)]
        return lax.ppermute(value, "tm", pairs + [(j, i) for i, j in pairs])

    big = ((ROWS, SHARE), BF16)
    state = ((HEADS, ROWS, LANES), F32)
    mine = jnp.concatenate([inputs, cotangent[:EDGE], cotangent[ROWS - EDGE:]], axis=0)
    mp = over_head(mine)
    b0 = over_b(mine)
    a0 = over_a(mine)
    b1 = over_b(mp)
    a1 = over_a(mp)
    cot_p = over_head(cotangent)
    taps_p = over_head(kernel)
    q, k, v = call(
        own_kernel, (info, inputs, mp, w_query, w_key, w_value), (big, big, big), us=2.0
    )
    ka, va, e_one, acc, top, total = call(
        first_kernel,
        (info, a0, a1, w_key, w_value, q, k, v),
        (big, big, ((HEADS, ROWS, 2 * ROWS), BF16), ((ROWS, SHARE), F32), state, state),
        us=4.0,
    )
    kb, vb, e_two, weight, att, part, edge_a, edge_b = call(
        second_kernel,
        (info, b0, b1, w_key, w_value, w_out, q, acc, top, total),
        (
            big,
            big,
            ((HEADS, ROWS, ROWS), BF16),
            ((2, HEADS, ROWS, LANES), F32),
            big,
            ((ROWS, D), BF16),
            ((EDGE, D), BF16),
            ((EDGE, D), BF16),
        ),
        us=4.0,
    )
    part_p = over_head(part)
    eb = over_b(edge_b)
    ea = over_a(edge_a)
    e2 = over_head(jnp.concatenate([eb, ea], axis=0))
    chunked = ((CHUNKS, EXT, LANES), F32)
    tall = ((ROWS, LANES), F32)
    output, dh, datt, gk = call(
        conv_kernel,
        (
            info, inputs, mp, a0, a1, b0, b1, part, part_p, ea, eb, e2, cotangent, cot_p,
            kernel, taps_p, w_out,
        ),
        (big, ((ROWS, SHARE), F32), big, ((KW, SHARE), F32)),
        scratch=(
            chunked, chunked, chunked, ((CHUNKS, ROWS, LANES), F32), ((ROWS, SHARE), F32),
            ((CHUNKS, 16, LANES), F32), tall, tall, tall, ((ROWS, D), BF16),
        ),
        us=6.0,
    )
    pair = ((2, ROWS, SHARE), BF16)
    dq_b, dkv_b = call(
        back_b_kernel,
        (q, kb, vb, datt, att, e_two, weight),
        (((ROWS, SHARE), F32), pair),
        smem=False,
        us=3.0,
    )
    got_b = over_b(dkv_b)
    dkv_a, dkv, pin = call(
        back_own_kernel,
        (info, q, k, v, ka, va, datt, att, e_one, weight, dq_b, w_query),
        (pair, ((2, ROWS, SHARE), F32), ((ROWS, D), F32)),
        us=6.0,
    )
    got_a = over_a(dkv_a)
    send, keep, stat = call(
        project_kernel,
        (info, inputs, mp, dkv, got_a, got_b, pin, w_key, w_value),
        (((ROWS, SHARE + LANES), BF16), ((ROWS, SHARE), F32), tall),
        us=2.0,
    )
    got = over_head(send)
    (grad,) = call(
        final_kernel, (inputs, mp, keep, stat, got, dh), (big,), smem=False, us=1.0
    )
    step = 1
    while step < count:
        gk = gk + lax.ppermute(gk, "tm", [(i, i ^ step) for i in range(count)])
        step *= 2
    return output, grad, gk


def solution(mesh):
    placed = (
        P("tm", "head"),
        P(None, "head"),
        P(None, "head"),
        P(None, "head"),
        P("head", None),
        P(None, "head"),
        P("tm", "head"),
    )
    return jax.shard_map(
        local,
        mesh=mesh,
        in_specs=placed,
        out_specs=(P("tm", "head"), P("tm", "head"), P(None, "head")),
        check_vma=False,
    )
```

```python
import functools
import jax
import jax.numpy as jnp
from jax import lax
from jax.experimental import pallas as pl
from jax.experimental.pallas import tpu as pltpu
from jax.sharding import PartitionSpec as P

D = 1024
HEAD_DIM = 128
BLOCK = 128
CONTEXT = 2
KW = 9
EPSILON = 1e-05
MASKED = -1e30

ROWS = CONTEXT * BLOCK
SHARE = 512
HEADS = SHARE // HEAD_DIM
LANES = 128
EDGE = 16
CHUNKS = D // LANES
HALF_CHUNKS = SHARE // LANES
PAD = 16
EXT = ROWS + 2 * PAD
HALF = KW // 2
SCALE = HEAD_DIM ** (-0.5)
F32 = jnp.float32
BF16 = jnp.bfloat16


def nn(a, b):
    return lax.dot_general(a, b, (((1,), (0,)), ((), ())), preferred_element_type=F32)


def nt(a, b):
    return lax.dot_general(a, b, (((1,), (1,)), ((), ())), preferred_element_type=F32)


def tn(a, b):
    return lax.dot_general(a, b, (((0,), (0,)), ((), ())), preferred_element_type=F32)


def row_sum(a):
    return jnp.sum(a, axis=1, keepdims=True)


def moments(a, b):
    center = (row_sum(a) + row_sum(b)) * (1.0 / D)
    spread = (row_sum(a * a) + row_sum(b * b)) * (1.0 / D) - center * center
    return center, lax.rsqrt(spread + EPSILON)


def norm_pair(a, b):
    a = a.astype(F32)
    b = b.astype(F32)
    center, rstd = moments(a, b)
    return (a - center) * rstd, (b - center) * rstd, rstd


def placement():
    place = lax.axis_index("tm")
    last = lax.axis_size("tm") - 1
    odd = lax.rem(place, 2)
    left = (place > 0).astype(jnp.int32)
    right = (place < last).astype(jnp.int32)
    return odd, left, right


def own_other():
    h = lax.axis_index("head")
    own = pl.ds(pl.multiple_of(h * SHARE, SHARE), SHARE)
    other = pl.ds(pl.multiple_of((1 - h) * SHARE, SHARE), SHARE)
    return own, other


def lanes_of(head):
    return slice(head * HEAD_DIM, (head + 1) * HEAD_DIM)


def band_bias(right, valid):
    row = (lax.broadcasted_iota(jnp.int32, (ROWS, ROWS), 0) >= BLOCK).astype(jnp.int32)
    col = (lax.broadcasted_iota(jnp.int32, (ROWS, ROWS), 1) >= BLOCK).astype(jnp.int32)
    hidden = ((row - col) == 1 - 2 * right) | (valid == 0)
    return jnp.where(hidden, MASKED, 0.0).astype(F32)


def own_kernel(xo, xp, wq, wk, wv, q, k, v):
    own, other = own_other()
    no, np_, _ = norm_pair(xo[...], xp[...])
    no = no.astype(BF16)
    np_ = np_.astype(BF16)
    for w, out in ((wq, q), (wk, k), (wv, v)):
        out[...] = (nn(no, w[own, :]) + nn(np_, w[other, :])).astype(BF16)


def halo_kv(xo, xp, wk, wv, k, v):
    own, other = own_other()
    no, np_, _ = norm_pair(xo[...], xp[...])
    no = no.astype(BF16)
    np_ = np_.astype(BF16)
    for w, out in ((wk, k), (wv, v)):
        out[...] = (nn(no, w[own, :]) + nn(np_, w[other, :])).astype(BF16)


def first_kernel(xo, xp, wk, wv, q, k, v, pack, ka, va, e, acc, top, total):
    halo_kv(xo, xp, wk, wv, ka, va)
    odd, _, _ = placement()
    bias = band_bias(1 - odd, 1)
    for head in range(HEADS):
        f = lanes_of(head)
        qh = q[:, f]
        s_own = nt(qh, k[:, f]) * SCALE
        s_a = nt(qh, ka[:, f]) * SCALE + bias
        m = jnp.maximum(jnp.max(s_own, axis=1, keepdims=True), jnp.max(s_a, axis=1, keepdims=True))
        e_own = jnp.exp(s_own - m)
        e_a = jnp.exp(s_a - m)
        total[head] = jnp.broadcast_to(row_sum(e_own) + row_sum(e_a), (ROWS, LANES))
        top[head] = jnp.broadcast_to(m, (ROWS, LANES))
        e_own = e_own.astype(BF16)
        e_a = e_a.astype(BF16)
        e[head, :, :ROWS] = e_own
        e[head, :, ROWS:] = e_a
        acc[:, f] = nn(e_own, v[:, f]) + nn(e_a, va[:, f])


def second_kernel(
    xo, xp, wk, wv, wo, q, acc, top, total, kb, vb, e, weight, att, edges
):
    halo_kv(xo, xp, wk, wv, kb, vb)
    odd, left, right = placement()
    bias = band_bias(odd, jnp.where(odd == 1, right, left))
    for head in range(HEADS):
        f = lanes_of(head)
        s = nt(q[:, f], kb[:, f]) * SCALE + bias
        m1 = top[head][:, :1]
        m = jnp.maximum(m1, jnp.max(s, axis=1, keepdims=True))
        shrink = jnp.exp(m1 - m)
        eb = jnp.exp(s - m)
        inverse = 1.0 / (total[head][:, :1] * shrink + row_sum(eb))
        eb = eb.astype(BF16)
        e[head] = eb
        o = (acc[:, f] * shrink + nn(eb, vb[:, f])) * inverse
        att[:, f] = o.astype(BF16)
        weight[0, head] = jnp.broadcast_to(shrink * inverse, (ROWS, LANES))
        weight[1, head] = jnp.broadcast_to(inverse, (ROWS, LANES))
    own, other = own_other()
    rim = jnp.concatenate([att[at, :] for at in edge_rows(placement()[0])], axis=0)
    edges[:, :SHARE] = nn(rim, wo[:, own]).astype(BF16)
    edges[:, SHARE:] = nn(rim, wo[:, other]).astype(BF16)


def project_out_kernel(att, wo, part):
    own, other = own_other()
    part[:, :SHARE] = nn(att[...], wo[:, own]).astype(BF16)
    part[:, SHARE:] = nn(att[...], wo[:, other]).astype(BF16)


def edge_rows(odd):
    last = ROWS - EDGE
    return (
        pl.ds(pl.multiple_of((1 - odd) * last, EDGE), EDGE),
        pl.ds(pl.multiple_of(odd * last, EDGE), EDGE),
    )


def merge_kernel(edges, edges_p, co, cp, to_a, to_b):
    for n, (at, out) in enumerate(zip(edge_rows(placement()[0]), (to_a, to_b))):
        rows = slice(n * EDGE, (n + 1) * EDGE)
        mine = edges[rows, :].astype(F32)
        theirs = edges_p[rows, :].astype(F32)
        out[:EDGE, :SHARE] = (mine[:, :SHARE] + theirs[:, SHARE:]).astype(BF16)
        out[:EDGE, SHARE:] = (mine[:, SHARE:] + theirs[:, :SHARE]).astype(BF16)
        out[EDGE:, :SHARE] = co[at, :]
        out[EDGE:, SHARE:] = cp[at, :]


def conv_kernel(
    xo, xp, a0, a1, b0, b1, part, part_p, ea, eb, co, cp, to, wo,
    output, dh, datt, gk,
    n2s, cs, dzs, dns, hs, taps, rs2, sum0, sum1, dhb,
):
    odd, left, right = placement()
    own, other = own_other()
    is_odd = odd == 1
    step = 32
    tp = unpack_taps(cp)
    for c in range(HALF_CHUNKS):
        f = slice(c * LANES, (c + 1) * LANES)
        taps[c, :KW, :] = to[:, f]
        taps[HALF_CHUNKS + c, :KW, :] = tp[:, f]

    def rows_in(index, carry):
        r = pl.multiple_of(index * step, step)
        rows = pl.ds(r, step)
        held = pl.ds(pl.multiple_of(PAD + r, PAD), step)
        p = part[rows, :].astype(F32)
        pp = part_p[rows, :].astype(F32)
        ho = xo[rows, :].astype(F32) + p[:, :SHARE] + pp[:, SHARE:]
        hp = xp[rows, :].astype(F32) + p[:, SHARE:] + pp[:, :SHARE]
        center, rstd = moments(ho, hp)
        hs[rows, :] = ho
        rs2[rows, :] = jnp.broadcast_to(rstd, (step, LANES))
        ctan = co[rows, :].astype(F32)
        ctan_p = cp[rows, :].astype(F32)
        for c in range(HALF_CHUNKS):
            f = slice(c * LANES, (c + 1) * LANES)
            n2s[c, held, :] = (ho[:, f] - center) * rstd
            n2s[HALF_CHUNKS + c, held, :] = (hp[:, f] - center) * rstd
            cs[c, held, :] = ctan[:, f]
            cs[HALF_CHUNKS + c, held, :] = ctan_p[:, f]
        return carry

    lax.fori_loop(0, ROWS // step, rows_in, 0)

    pa = ea[:EDGE, :].astype(F32)
    pb = eb[:EDGE, :].astype(F32)
    sides = (
        (slice(ROWS - EDGE, ROWS), is_odd, 0, left),
        (slice(0, EDGE), jnp.logical_not(is_odd), PAD + ROWS, right),
    )
    for x_rows, from_a, at, valid in sides:
        def pick(one, two):
            return jnp.where(from_a, one.astype(F32), two.astype(F32))

        pe = pick(pa, pb)
        ho = pick(a0[x_rows, :], b0[x_rows, :]) + pe[:, :SHARE]
        hp = pick(a1[x_rows, :], b1[x_rows, :]) + pe[:, SHARE:]
        center, rstd = moments(ho, hp)
        ctan = pick(ea[EDGE:, :SHARE], eb[EDGE:, :SHARE])
        ctan_p = pick(ea[EDGE:, SHARE:], eb[EDGE:, SHARE:])
        inside = valid == 1
        for c in range(HALF_CHUNKS):
            f = slice(c * LANES, (c + 1) * LANES)
            for d, hh, cc in ((c, ho, ctan), (HALF_CHUNKS + c, hp, ctan_p)):
                n2s[d, at:at + EDGE, :] = jnp.where(inside, (hh[:, f] - center) * rstd, 0.0)
                cs[d, at:at + EDGE, :] = jnp.where(inside, cc[:, f], 0.0)

    piece = 136

    def forward(c, carry, mine):
        w = taps[c]
        for r0 in (8, 8 + piece):
            z = w[0:1, :] * n2s[c, r0 - HALF:r0 - HALF + piece, :]
            for tap in range(1, KW):
                at = r0 + tap - HALF
                z = z + w[tap:tap + 1, :] * n2s[c, at:at + piece, :]
            gate = jax.nn.sigmoid(z)
            dzs[c, r0:r0 + piece, :] = cs[c, r0:r0 + piece, :] * gate * (1.0 + z * (1.0 - gate))
            if mine:
                lo = max(r0, PAD)
                hi = min(r0 + piece, PAD + ROWS)
                lane = pl.ds(pl.multiple_of(c * LANES, LANES), LANES)
                mix = (z * gate)[lo - r0:hi - r0, :]
                hs[lo - PAD:hi - PAD, lane] = hs[lo - PAD:hi - PAD, lane] + mix
        if mine:
            lane = pl.ds(pl.multiple_of(c * LANES, LANES), LANES)
            dz = dzs[c, PAD:PAD + ROWS, :]
            for tap in range(KW):
                at = PAD + tap - HALF
                gk[tap:tap + 1, lane] = jnp.sum(
                    dz * n2s[c, at:at + ROWS, :], axis=0, keepdims=True
                )
        return carry

    lax.fori_loop(0, HALF_CHUNKS, functools.partial(forward, mine=True), 0)
    lax.fori_loop(HALF_CHUNKS, CHUNKS, functools.partial(forward, mine=False), 0)
    output[...] = hs[...].astype(BF16)

    sum0[...] = jnp.zeros_like(sum0)
    sum1[...] = jnp.zeros_like(sum1)

    def backward(c, carry):
        w = taps[c]
        for r0 in (0, ROWS // 2):
            at = PAD + r0 + HALF
            g = w[0:1, :] * dzs[c, at:at + ROWS // 2, :]
            for tap in range(1, KW):
                at = PAD + r0 + HALF - tap
                g = g + w[tap:tap + 1, :] * dzs[c, at:at + ROWS // 2, :]
            dns[c, r0:r0 + ROWS // 2, :] = g
            half = slice(r0, r0 + ROWS // 2)
            sum0[half, :] = sum0[half, :] + g
            sum1[half, :] = sum1[half, :] + g * n2s[c, PAD + r0:PAD + r0 + ROWS // 2, :]
        return carry

    lax.fori_loop(0, CHUNKS, backward, 0)
    sum0[...] = jnp.broadcast_to(row_sum(sum0[...]) * (1.0 / D), (ROWS, LANES))
    sum1[...] = jnp.broadcast_to(row_sum(sum1[...]) * (1.0 / D), (ROWS, LANES))

    def finish(c, carry, mine):
        lane = pl.ds(pl.multiple_of(c * LANES, LANES), LANES)
        value = cs[c, PAD:PAD + ROWS, :] + rs2[...] * (
            dns[c] - sum0[...] - n2s[c, PAD:PAD + ROWS, :] * sum1[...]
        )
        if mine:
            dh[:, lane] = value
        dhb[:, lane] = value.astype(BF16)
        return carry

    lax.fori_loop(0, HALF_CHUNKS, functools.partial(finish, mine=True), 0)
    lax.fori_loop(HALF_CHUNKS, CHUNKS, functools.partial(finish, mine=False), 0)
    datt[...] = (nt(dhb[:, :SHARE], wo[:, own]) + nt(dhb[:, SHARE:], wo[:, other])).astype(BF16)


def pair_grad(qh, kh, vh, gh, eh, wh, delta):
    dots = nt(gh, vh)
    p = eh.astype(F32) * wh
    ds = (p * (dots - delta) * SCALE).astype(BF16)
    return nn(ds, kh), tn(ds, qh), tn(p.astype(BF16), gh)


def back_halo_kernel(q, k, v, datt, att, e, weight, *refs, which):
    dq, dkv = refs[-2:]
    at = pl.ds(ROWS, ROWS) if which == 0 else pl.ds(0, ROWS)
    for head in range(HEADS):
        f = lanes_of(head)
        gh = datt[:, f]
        delta = row_sum(gh.astype(F32) * att[:, f].astype(F32))
        d_q, d_k, d_v = pair_grad(
            q[:, f], k[:, f], v[:, f], gh, e[head, :, at], weight[which, head][:, :1], delta
        )
        dq[:, f] = d_q + refs[0][:, f] if which == 0 else d_q
        dkv[0, :, f] = d_k.astype(BF16)
        dkv[1, :, f] = d_v.astype(BF16)


def back_own_kernel(q, k, v, datt, att, e, weight, dq_ab, wq, after, dkv, pin):
    dq = []
    for head in range(HEADS):
        f = lanes_of(head)
        gh = datt[:, f]
        delta = row_sum(gh.astype(F32) * att[:, f].astype(F32))
        d_q, d_k, d_v = pair_grad(
            q[:, f], k[:, f], v[:, f], gh, e[head, :, :ROWS], weight[0, head][:, :1], delta
        )
        dkv[0, :, f] = d_k
        dkv[1, :, f] = d_v
        dq.append((d_q + dq_ab[:, f]).astype(BF16))
    own, other = own_other()
    dq = jnp.concatenate(dq, axis=1)
    pin[:, :SHARE] = nt(dq, wq[own, :])
    pin[:, SHARE:] = nt(dq, wq[other, :])


def project_kernel(xo, xp, dkv, got_a, got_b, pin, wk, wv, after, send, keep, stat):
    own, other = own_other()
    dk = (dkv[0] + got_a[0].astype(F32) + got_b[0].astype(F32)).astype(BF16)
    dv = (dkv[1] + got_a[1].astype(F32) + got_b[1].astype(F32)).astype(BF16)
    p_own = pin[:, :SHARE] + nt(dk, wk[own, :]) + nt(dv, wv[own, :])
    p_other = pin[:, SHARE:] + nt(dk, wk[other, :]) + nt(dv, wv[other, :])
    no, np_, _ = norm_pair(xo[...], xp[...])
    s0 = row_sum(p_own) + row_sum(p_other)
    s1 = row_sum(p_own * no) + row_sum(p_other * np_)
    keep[...] = p_own
    send[:, :SHARE] = p_other.astype(BF16)
    lane = lax.broadcasted_iota(jnp.int32, (ROWS, LANES), 1)
    s0_hi = s0.astype(BF16).astype(F32)
    s1_hi = s1.astype(BF16).astype(F32)
    packed = jnp.where(lane == 0, s0_hi, 0.0)
    packed = jnp.where(lane == 1, s0 - s0_hi, packed)
    packed = jnp.where(lane == 2, s1_hi, packed)
    packed = jnp.where(lane == 3, s1 - s1_hi, packed)
    send[:, SHARE:] = packed.astype(BF16)
    stat[...] = jnp.where(lane == 0, s0, jnp.where(lane == 2, s1, 0.0))


def final_kernel(xo, xp, keep, stat, got, dh, after, grad):
    no, _, rstd = norm_pair(xo[...], xp[...])
    dn1 = keep[...] + got[:, :SHARE].astype(F32)
    lane = lax.broadcasted_iota(jnp.int32, (ROWS, LANES), 1)
    sums = stat[...] + got[:, SHARE:].astype(F32)
    s0 = row_sum(jnp.where(lane < 2, sums, 0.0)) * (1.0 / D)
    s1 = row_sum(jnp.where(lane < 2, 0.0, sums)) * (1.0 / D)
    grad[...] = (dh[...] + rstd * (dn1 - s0 - no * s1)).astype(BF16)


def sum_kernel(*refs):
    refs[-1][...] = sum(ref[...] for ref in refs[:-1])


def stage_kernel(*refs):
    half = (len(refs) - 2) // 2
    pack, sems = refs[-2:]
    copies = [
        pltpu.make_async_copy(refs[i], refs[half + i], sems.at[i]) for i in range(half)
    ]
    for copy in copies:
        copy.start()
    for copy in copies:
        copy.wait()
    co, taps = refs[2 * half - 2:2 * half]
    pack[:ROWS, :] = co[...]
    rest = taps[...]
    for n in range(3):
        piece = rest.astype(BF16)
        pack[ROWS + n * EDGE:ROWS + n * EDGE + KW, :] = piece
        rest = rest - piece.astype(F32)


def unpack_taps(pack):
    return sum(
        pack[ROWS + n * EDGE:ROWS + n * EDGE + KW, :].astype(F32) for n in (2, 1, 0)
    )


def stage(*arrays):
    outs = [pltpu.VMEM(a.shape, a.dtype) for a in arrays]
    outs.append(pltpu.VMEM((ROWS + 3 * EDGE, SHARE), BF16))
    return pl.pallas_call(
        stage_kernel,
        out_shape=outs,
        in_specs=[pl.BlockSpec(memory_space=pltpu.HBM)] * len(arrays),
        out_specs=[pl.BlockSpec(memory_space=pltpu.VMEM)] * len(outs),
        scratch_shapes=[pltpu.SemaphoreType.DMA((len(arrays),))],
        compiler_params=pltpu.CompilerParams(vmem_limit_bytes=6 * 1024 * 1024),
        cost_estimate=pl.CostEstimate(flops=0, bytes_accessed=64 * 1024 * 1024, transcendentals=0),
    )(*[pltpu.with_memory_space_constraint(a, pltpu.HBM) for a in arrays])


def call(kernel, args, outs, scratch=(), us=1.0, mib=6):
    whole = pl.BlockSpec(memory_space=pltpu.VMEM)
    return pl.pallas_call(
        kernel,
        out_shape=[jax.ShapeDtypeStruct(shape, dtype) for shape, dtype in outs],
        in_specs=[whole] * len(args),
        out_specs=[whole] * len(outs),
        scratch_shapes=[pltpu.VMEM(shape, dtype) for shape, dtype in scratch],
        compiler_params=pltpu.CompilerParams(vmem_limit_bytes=mib * 1024 * 1024),
        cost_estimate=pl.CostEstimate(
            flops=int(us * 1e10), bytes_accessed=int(us * 1e7), transcendentals=0
        ),
    )(*args)


def local(inputs, w_query, w_key, w_value, w_out, kernel, cotangent):
    count = lax.axis_size("tm")
    assert inputs.shape == (ROWS, SHARE) and count % 2 == 0
    def over_head(value):
        return lax.ppermute(value, "head", [(0, 1), (1, 0)])

    def over_a(value):
        return lax.ppermute(value, "tm", [(i, i ^ 1) for i in range(count)])

    def over_b(value):
        pairs = [(i, i + 1) for i in range(1, count - 1, 2)]
        return lax.ppermute(value, "tm", pairs + [(j, i) for i, j in pairs])

    big = ((ROWS, SHARE), BF16)
    state = ((HEADS, ROWS, LANES), F32)
    xp = over_head(inputs)
    b0 = over_b(inputs)
    a0 = over_a(inputs)
    *staged, pack = stage(w_query, w_key, w_value, w_out, inputs, cotangent, kernel)
    pack_p = over_head(pack)
    xp, a0, b0, *staged = lax.optimization_barrier((xp, a0, b0, *staged))
    w_query, w_key, w_value, w_out, inputs, cotangent, kernel = staged
    b1 = over_b(xp)
    a1 = over_a(xp)
    q, k, v = call(
        own_kernel, (inputs, xp, w_query, w_key, w_value), (big, big, big), us=2.0
    )
    ka, va, e_one, acc, top, total = call(
        first_kernel,
        (a0, a1, w_key, w_value, q, k, v, pack_p),
        (big, big, ((HEADS, ROWS, 2 * ROWS), BF16), ((ROWS, SHARE), F32), state, state),
        us=3.0,
    )
    edge = ((2 * EDGE, D), BF16)
    kb, vb, e_two, weight, att, edges = call(
        second_kernel,
        (b0, b1, w_key, w_value, w_out, q, acc, top, total),
        (
            big,
            big,
            ((HEADS, ROWS, ROWS), BF16),
            ((2, HEADS, ROWS, LANES), F32),
            big,
            edge,
        ),
        us=4.0,
    )
    edges_p = over_head(edges)
    (part,) = call(project_out_kernel, (att, w_out), (((ROWS, D), BF16),), us=1.0)
    part_p = over_head(part)
    to_a, to_b = call(
        merge_kernel, (edges, edges_p, cotangent, pack_p), (edge, edge), us=3.0
    )
    eb = over_b(to_b)
    ea = over_a(to_a)
    chunked = ((CHUNKS, EXT, LANES), F32)
    tall = ((ROWS, LANES), F32)
    output, dh, datt, gk = call(
        conv_kernel,
        (
            inputs, xp, a0, a1, b0, b1, part, part_p, ea, eb, cotangent, pack_p,
            kernel, w_out,
        ),
        (big, ((ROWS, SHARE), F32), big, ((KW, SHARE), F32)),
        scratch=(
            chunked, chunked, chunked, ((CHUNKS, ROWS, LANES), F32), ((ROWS, SHARE), F32),
            ((CHUNKS, 16, LANES), F32), tall, tall, tall, ((ROWS, D), BF16),
        ),
        us=5.0,
        mib=12,
    )
    chain = [gk]
    assert count == 128
    for steps in ((1,), (8, 16, 24), (32, 64, 96), (2, 4, 6)):
        last = chain[-1]
        parts = [
            lax.ppermute(last, "tm", [(i, i ^ step) for i in range(count)]) for step in steps
        ]
        chain.extend(call(sum_kernel, (last, *parts), (((KW, SHARE), F32),), us=0.2, mib=1))
    pair = ((2, ROWS, SHARE), BF16)
    dq_b, dkv_b = call(
        functools.partial(back_halo_kernel, which=1),
        (q, kb, vb, datt, att, e_two, weight),
        (((ROWS, SHARE), F32), pair),
        us=1.5,
    )
    got_b = over_b(dkv_b)
    dq_ab, dkv_a = call(
        functools.partial(back_halo_kernel, which=0),
        (q, ka, va, datt, att, e_one, weight, dq_b, chain[1]),
        (((ROWS, SHARE), F32), pair),
        us=1.5,
    )
    got_a = over_a(dkv_a)
    dkv, pin = call(
        back_own_kernel,
        (q, k, v, datt, att, e_one, weight, dq_ab, w_query, chain[1]),
        (((2, ROWS, SHARE), F32), ((ROWS, D), F32)),
        us=2.0,
    )
    send, keep, stat = call(
        project_kernel,
        (inputs, xp, dkv, got_a, got_b, pin, w_key, w_value, chain[2]),
        (((ROWS, SHARE + LANES), BF16), ((ROWS, SHARE), F32), tall),
        us=1.5,
    )
    got = over_head(send)
    (grad,) = call(
        final_kernel, (inputs, xp, keep, stat, got, dh, chain[3]), (big,), us=1.0
    )
    return output, grad, chain[-1]


def solution(mesh):
    placed = (
        P("tm", "head"),
        P(None, "head"),
        P(None, "head"),
        P(None, "head"),
        P("head", None),
        P(None, "head"),
        P("tm", "head"),
    )
    return jax.shard_map(
        local,
        mesh=mesh,
        in_specs=placed,
        out_specs=(P("tm", "head"), P("tm", "head"), P(None, "head")),
        check_vma=False,
    )
```

```python
import functools
import jax
import jax.numpy as jnp
from jax import lax
from jax.experimental import pallas as pl
from jax.experimental.pallas import tpu as pltpu
from jax.sharding import PartitionSpec as P

D = 1024
HEAD_DIM = 128
BLOCK = 128
CONTEXT = 2
KW = 9
EPSILON = 1e-05
MASKED = -1e30

ROWS = CONTEXT * BLOCK
SHARE = 512
HEADS = SHARE // HEAD_DIM
LANES = 128
EDGE = 16
CHUNKS = D // LANES
HALF_CHUNKS = SHARE // LANES
PAD = 16
EXT = ROWS + 2 * PAD
HALF = KW // 2
SCALE = HEAD_DIM ** (-0.5)
F32 = jnp.float32
BF16 = jnp.bfloat16


def nn(a, b):
    return lax.dot_general(a, b, (((1,), (0,)), ((), ())), preferred_element_type=F32)


def nt(a, b):
    return lax.dot_general(a, b, (((1,), (1,)), ((), ())), preferred_element_type=F32)


def tn(a, b):
    return lax.dot_general(a, b, (((0,), (0,)), ((), ())), preferred_element_type=F32)


def row_sum(a):
    return jnp.sum(a, axis=1, keepdims=True)


def moments(a, b):
    center = (row_sum(a) + row_sum(b)) * (1.0 / D)
    spread = (row_sum(a * a) + row_sum(b * b)) * (1.0 / D) - center * center
    return center, lax.rsqrt(spread + EPSILON)


def norm_pair(a, b):
    a = a.astype(F32)
    b = b.astype(F32)
    center, rstd = moments(a, b)
    return (a - center) * rstd, (b - center) * rstd, rstd


def placement():
    place = lax.axis_index("tm")
    last = lax.axis_size("tm") - 1
    odd = lax.rem(place, 2)
    left = (place > 0).astype(jnp.int32)
    right = (place < last).astype(jnp.int32)
    return odd, left, right


def own_other():
    h = lax.axis_index("head")
    own = pl.ds(pl.multiple_of(h * SHARE, SHARE), SHARE)
    other = pl.ds(pl.multiple_of((1 - h) * SHARE, SHARE), SHARE)
    return own, other


def lanes_of(head):
    return slice(head * HEAD_DIM, (head + 1) * HEAD_DIM)


def band_bias(right, valid):
    row = (lax.broadcasted_iota(jnp.int32, (ROWS, ROWS), 0) >= BLOCK).astype(jnp.int32)
    col = (lax.broadcasted_iota(jnp.int32, (ROWS, ROWS), 1) >= BLOCK).astype(jnp.int32)
    hidden = ((row - col) == 1 - 2 * right) | (valid == 0)
    return jnp.where(hidden, MASKED, 0.0).astype(F32)


def own_kernel(xo, xp, wq, wk, wv, q, k, v):
    own, other = own_other()
    no, np_, _ = norm_pair(xo[...], xp[...])
    no = no.astype(BF16)
    np_ = np_.astype(BF16)
    for w, out in ((wq, q), (wk, k), (wv, v)):
        out[...] = (nn(no, w[own, :]) + nn(np_, w[other, :])).astype(BF16)


def halo_kv(xo, xp, wk, wv, k, v):
    own, other = own_other()
    no, np_, _ = norm_pair(xo[...], xp[...])
    no = no.astype(BF16)
    np_ = np_.astype(BF16)
    for w, out in ((wk, k), (wv, v)):
        out[...] = (nn(no, w[own, :]) + nn(np_, w[other, :])).astype(BF16)


def attend_kernel(a0, a1, b0, b1, wk, wv, wo, q, k, v, ka, va, kb, vb, p, att, edges):
    halo_kv(a0, a1, wk, wv, ka, va)
    halo_kv(b0, b1, wk, wv, kb, vb)
    odd, left, right = placement()
    bias_a = band_bias(1 - odd, 1)
    bias_b = band_bias(odd, jnp.where(odd == 1, right, left))
    for head in range(HEADS):
        f = lanes_of(head)
        qh = q[:, f]
        scores = (
            nt(qh, k[:, f]) * SCALE,
            nt(qh, ka[:, f]) * SCALE + bias_a,
            nt(qh, kb[:, f]) * SCALE + bias_b,
        )
        top = functools.reduce(jnp.maximum, scores)
        top = jnp.max(top, axis=1, keepdims=True)
        scores = [jnp.exp(s - top) for s in scores]
        inverse = 1.0 / row_sum(sum(scores))
        out = 0.0
        for n, (s, values) in enumerate(zip(scores, (v, va, vb))):
            s = (s * inverse).astype(BF16)
            p[head, :, n * ROWS:(n + 1) * ROWS] = s
            out = out + nn(s, values[:, f])
        att[:, f] = out.astype(BF16)
    own, other = own_other()
    rim = jnp.concatenate([att[at, :] for at in edge_rows(odd)], axis=0)
    edges[:, :SHARE] = nn(rim, wo[:, own]).astype(BF16)
    edges[:, SHARE:] = nn(rim, wo[:, other]).astype(BF16)


def project_out_kernel(att, wo, part):
    own, other = own_other()
    part[:, :SHARE] = nn(att[...], wo[:, own]).astype(BF16)
    part[:, SHARE:] = nn(att[...], wo[:, other]).astype(BF16)


def edge_rows(odd):
    last = ROWS - EDGE
    return (
        pl.ds(pl.multiple_of((1 - odd) * last, EDGE), EDGE),
        pl.ds(pl.multiple_of(odd * last, EDGE), EDGE),
    )


def merge_kernel(edges, edges_p, co, cp, to_a, to_b):
    for n, (at, out) in enumerate(zip(edge_rows(placement()[0]), (to_a, to_b))):
        rows = slice(n * EDGE, (n + 1) * EDGE)
        mine = edges[rows, :].astype(F32)
        theirs = edges_p[rows, :].astype(F32)
        out[:EDGE, :SHARE] = (mine[:, :SHARE] + theirs[:, SHARE:]).astype(BF16)
        out[:EDGE, SHARE:] = (mine[:, SHARE:] + theirs[:, :SHARE]).astype(BF16)
        out[EDGE:, :SHARE] = co[at, :]
        out[EDGE:, SHARE:] = cp[at, :]


def conv_kernel(
    xo, xp, a0, a1, b0, b1, part, part_p, ea, eb, co, cp, to, wo,
    output, dh, datt, gk,
    n2s, cs, dzs, dns, hs, taps, rs2, sum0, sum1, dhb,
):
    odd, left, right = placement()
    own, other = own_other()
    is_odd = odd == 1
    step = 32
    tp = unpack_taps(cp)
    for c in range(HALF_CHUNKS):
        f = slice(c * LANES, (c + 1) * LANES)
        taps[c, :KW, :] = to[:, f]
        taps[HALF_CHUNKS + c, :KW, :] = tp[:, f]

    def rows_in(index, carry):
        r = pl.multiple_of(index * step, step)
        rows = pl.ds(r, step)
        held = pl.ds(pl.multiple_of(PAD + r, PAD), step)
        p = part[rows, :].astype(F32)
        pp = part_p[rows, :].astype(F32)
        ho = xo[rows, :].astype(F32) + p[:, :SHARE] + pp[:, SHARE:]
        hp = xp[rows, :].astype(F32) + p[:, SHARE:] + pp[:, :SHARE]
        center, rstd = moments(ho, hp)
        hs[rows, :] = ho
        rs2[rows, :] = jnp.broadcast_to(rstd, (step, LANES))
        ctan = co[rows, :].astype(F32)
        ctan_p = cp[rows, :].astype(F32)
        for c in range(HALF_CHUNKS):
            f = slice(c * LANES, (c + 1) * LANES)
            n2s[c, held, :] = (ho[:, f] - center) * rstd
            n2s[HALF_CHUNKS + c, held, :] = (hp[:, f] - center) * rstd
            cs[c, held, :] = ctan[:, f]
            cs[HALF_CHUNKS + c, held, :] = ctan_p[:, f]
        return carry

    lax.fori_loop(0, ROWS // step, rows_in, 0)

    pa = ea[:EDGE, :].astype(F32)
    pb = eb[:EDGE, :].astype(F32)
    sides = (
        (slice(ROWS - EDGE, ROWS), is_odd, 0, left),
        (slice(0, EDGE), jnp.logical_not(is_odd), PAD + ROWS, right),
    )
    for x_rows, from_a, at, valid in sides:
        def pick(one, two):
            return jnp.where(from_a, one.astype(F32), two.astype(F32))

        pe = pick(pa, pb)
        ho = pick(a0[x_rows, :], b0[x_rows, :]) + pe[:, :SHARE]
        hp = pick(a1[x_rows, :], b1[x_rows, :]) + pe[:, SHARE:]
        center, rstd = moments(ho, hp)
        ctan = pick(ea[EDGE:, :SHARE], eb[EDGE:, :SHARE])
        ctan_p = pick(ea[EDGE:, SHARE:], eb[EDGE:, SHARE:])
        inside = valid == 1
        for c in range(HALF_CHUNKS):
            f = slice(c * LANES, (c + 1) * LANES)
            for d, hh, cc in ((c, ho, ctan), (HALF_CHUNKS + c, hp, ctan_p)):
                n2s[d, at:at + EDGE, :] = jnp.where(inside, (hh[:, f] - center) * rstd, 0.0)
                cs[d, at:at + EDGE, :] = jnp.where(inside, cc[:, f], 0.0)

    piece = 136

    def forward(c, carry, mine):
        w = taps[c]
        for r0 in (8, 8 + piece):
            z = w[0:1, :] * n2s[c, r0 - HALF:r0 - HALF + piece, :]
            for tap in range(1, KW):
                at = r0 + tap - HALF
                z = z + w[tap:tap + 1, :] * n2s[c, at:at + piece, :]
            gate = jax.nn.sigmoid(z)
            dzs[c, r0:r0 + piece, :] = cs[c, r0:r0 + piece, :] * gate * (1.0 + z * (1.0 - gate))
            if mine:
                lo = max(r0, PAD)
                hi = min(r0 + piece, PAD + ROWS)
                lane = pl.ds(pl.multiple_of(c * LANES, LANES), LANES)
                mix = (z * gate)[lo - r0:hi - r0, :]
                hs[lo - PAD:hi - PAD, lane] = hs[lo - PAD:hi - PAD, lane] + mix
        if mine:
            lane = pl.ds(pl.multiple_of(c * LANES, LANES), LANES)
            dz = dzs[c, PAD:PAD + ROWS, :]
            for tap in range(KW):
                at = PAD + tap - HALF
                gk[tap:tap + 1, lane] = jnp.sum(
                    dz * n2s[c, at:at + ROWS, :], axis=0, keepdims=True
                )
        return carry

    lax.fori_loop(0, HALF_CHUNKS, functools.partial(forward, mine=True), 0)
    lax.fori_loop(HALF_CHUNKS, CHUNKS, functools.partial(forward, mine=False), 0)
    output[...] = hs[...].astype(BF16)

    sum0[...] = jnp.zeros_like(sum0)
    sum1[...] = jnp.zeros_like(sum1)

    def backward(c, carry):
        w = taps[c]
        for r0 in (0, ROWS // 2):
            at = PAD + r0 + HALF
            g = w[0:1, :] * dzs[c, at:at + ROWS // 2, :]
            for tap in range(1, KW):
                at = PAD + r0 + HALF - tap
                g = g + w[tap:tap + 1, :] * dzs[c, at:at + ROWS // 2, :]
            dns[c, r0:r0 + ROWS // 2, :] = g
            half = slice(r0, r0 + ROWS // 2)
            sum0[half, :] = sum0[half, :] + g
            sum1[half, :] = sum1[half, :] + g * n2s[c, PAD + r0:PAD + r0 + ROWS // 2, :]
        return carry

    lax.fori_loop(0, CHUNKS, backward, 0)
    sum0[...] = jnp.broadcast_to(row_sum(sum0[...]) * (1.0 / D), (ROWS, LANES))
    sum1[...] = jnp.broadcast_to(row_sum(sum1[...]) * (1.0 / D), (ROWS, LANES))

    def finish(c, carry, mine):
        lane = pl.ds(pl.multiple_of(c * LANES, LANES), LANES)
        value = cs[c, PAD:PAD + ROWS, :] + rs2[...] * (
            dns[c] - sum0[...] - n2s[c, PAD:PAD + ROWS, :] * sum1[...]
        )
        if mine:
            dh[:, lane] = value
        dhb[:, lane] = value.astype(BF16)
        return carry

    lax.fori_loop(0, HALF_CHUNKS, functools.partial(finish, mine=True), 0)
    lax.fori_loop(HALF_CHUNKS, CHUNKS, functools.partial(finish, mine=False), 0)
    datt[...] = (nt(dhb[:, :SHARE], wo[:, own]) + nt(dhb[:, SHARE:], wo[:, other])).astype(BF16)


def pair_grad(qh, kh, vh, gh, p, delta):
    dots = nt(gh, vh)
    ds = (p.astype(F32) * (dots - delta) * SCALE).astype(BF16)
    return nn(ds, kh), tn(ds, qh), tn(p, gh)


def back_halo_kernel(q, k, v, datt, att, p, *refs, which):
    dq, dkv = refs[-2:]
    at = slice(which * ROWS, (which + 1) * ROWS)
    for head in range(HEADS):
        f = lanes_of(head)
        gh = datt[:, f]
        delta = row_sum(gh.astype(F32) * att[:, f].astype(F32))
        d_q, d_k, d_v = pair_grad(q[:, f], k[:, f], v[:, f], gh, p[head, :, at], delta)
        dq[:, f] = d_q + refs[0][:, f] if which == 1 else d_q
        dkv[0, :, f] = d_k.astype(BF16)
        dkv[1, :, f] = d_v.astype(BF16)


def back_own_kernel(q, k, v, datt, att, p, dq_ab, wq, after, dkv, pin):
    dq = []
    for head in range(HEADS):
        f = lanes_of(head)
        gh = datt[:, f]
        delta = row_sum(gh.astype(F32) * att[:, f].astype(F32))
        d_q, d_k, d_v = pair_grad(q[:, f], k[:, f], v[:, f], gh, p[head, :, :ROWS], delta)
        dkv[0, :, f] = d_k
        dkv[1, :, f] = d_v
        dq.append((d_q + dq_ab[:, f]).astype(BF16))
    own, other = own_other()
    dq = jnp.concatenate(dq, axis=1)
    pin[:, :SHARE] = nt(dq, wq[own, :])
    pin[:, SHARE:] = nt(dq, wq[other, :])


def project_kernel(xo, xp, dkv, got_a, got_b, pin, wk, wv, after, send, keep, stat):
    own, other = own_other()
    dk = (dkv[0] + got_a[0].astype(F32) + got_b[0].astype(F32)).astype(BF16)
    dv = (dkv[1] + got_a[1].astype(F32) + got_b[1].astype(F32)).astype(BF16)
    p_own = pin[:, :SHARE] + nt(dk, wk[own, :]) + nt(dv, wv[own, :])
    p_other = pin[:, SHARE:] + nt(dk, wk[other, :]) + nt(dv, wv[other, :])
    no, np_, _ = norm_pair(xo[...], xp[...])
    s0 = row_sum(p_own) + row_sum(p_other)
    s1 = row_sum(p_own * no) + row_sum(p_other * np_)
    keep[...] = p_own
    send[:, :SHARE] = p_other.astype(BF16)
    lane = lax.broadcasted_iota(jnp.int32, (ROWS, LANES), 1)
    s0_hi = s0.astype(BF16).astype(F32)
    s1_hi = s1.astype(BF16).astype(F32)
    packed = jnp.where(lane == 0, s0_hi, 0.0)
    packed = jnp.where(lane == 1, s0 - s0_hi, packed)
    packed = jnp.where(lane == 2, s1_hi, packed)
    packed = jnp.where(lane == 3, s1 - s1_hi, packed)
    send[:, SHARE:] = packed.astype(BF16)
    stat[...] = jnp.where(lane == 0, s0, jnp.where(lane == 2, s1, 0.0))


def final_kernel(xo, xp, keep, stat, got, dh, after, grad):
    no, _, rstd = norm_pair(xo[...], xp[...])
    dn1 = keep[...] + got[:, :SHARE].astype(F32)
    lane = lax.broadcasted_iota(jnp.int32, (ROWS, LANES), 1)
    sums = stat[...] + got[:, SHARE:].astype(F32)
    s0 = row_sum(jnp.where(lane < 2, sums, 0.0)) * (1.0 / D)
    s1 = row_sum(jnp.where(lane < 2, 0.0, sums)) * (1.0 / D)
    grad[...] = (dh[...] + rstd * (dn1 - s0 - no * s1)).astype(BF16)


def sum_kernel(*refs):
    refs[-1][...] = sum(ref[...] for ref in refs[:-1])


def stage_kernel(*refs):
    half = (len(refs) - 2) // 2
    pack, sems = refs[-2:]
    copies = [
        pltpu.make_async_copy(refs[i], refs[half + i], sems.at[i]) for i in range(half)
    ]
    for copy in copies:
        copy.start()
    for copy in copies:
        copy.wait()
    co, taps = refs[2 * half - 2:2 * half]
    pack[:ROWS, :] = co[...]
    rest = taps[...]
    for n in range(3):
        piece = rest.astype(BF16)
        pack[ROWS + n * EDGE:ROWS + n * EDGE + KW, :] = piece
        rest = rest - piece.astype(F32)


def unpack_taps(pack):
    return sum(
        pack[ROWS + n * EDGE:ROWS + n * EDGE + KW, :].astype(F32) for n in (2, 1, 0)
    )


def stage(*arrays):
    outs = [pltpu.VMEM(a.shape, a.dtype) for a in arrays]
    outs.append(pltpu.VMEM((ROWS + 3 * EDGE, SHARE), BF16))
    return pl.pallas_call(
        stage_kernel,
        out_shape=outs,
        in_specs=[pl.BlockSpec(memory_space=pltpu.HBM)] * len(arrays),
        out_specs=[pl.BlockSpec(memory_space=pltpu.VMEM)] * len(outs),
        scratch_shapes=[pltpu.SemaphoreType.DMA((len(arrays),))],
        compiler_params=pltpu.CompilerParams(vmem_limit_bytes=6 * 1024 * 1024),
        cost_estimate=pl.CostEstimate(flops=0, bytes_accessed=64 * 1024 * 1024, transcendentals=0),
    )(*[pltpu.with_memory_space_constraint(a, pltpu.HBM) for a in arrays])


def call(kernel, args, outs, scratch=(), us=1.0, mib=6):
    whole = pl.BlockSpec(memory_space=pltpu.VMEM)
    return pl.pallas_call(
        kernel,
        out_shape=[jax.ShapeDtypeStruct(shape, dtype) for shape, dtype in outs],
        in_specs=[whole] * len(args),
        out_specs=[whole] * len(outs),
        scratch_shapes=[pltpu.VMEM(shape, dtype) for shape, dtype in scratch],
        compiler_params=pltpu.CompilerParams(vmem_limit_bytes=mib * 1024 * 1024),
        cost_estimate=pl.CostEstimate(
            flops=int(us * 1e10), bytes_accessed=int(us * 1e7), transcendentals=0
        ),
    )(*args)


def local(inputs, w_query, w_key, w_value, w_out, kernel, cotangent):
    count = lax.axis_size("tm")
    assert inputs.shape == (ROWS, SHARE) and count % 2 == 0
    def over_head(value):
        return lax.ppermute(value, "head", [(0, 1), (1, 0)])

    def over_a(value):
        return lax.ppermute(value, "tm", [(i, i ^ 1) for i in range(count)])

    def over_b(value):
        pairs = [(i, i + 1) for i in range(1, count - 1, 2)]
        return lax.ppermute(value, "tm", pairs + [(j, i) for i, j in pairs])

    big = ((ROWS, SHARE), BF16)
    def over_b_and_head(value):
        pairs = [(i, i + 1) for i in range(1, count - 1, 2)]
        pairs = pairs + [(j, i) for i, j in pairs]
        crossed = [(2 * i + h, 2 * j + 1 - h) for i, j in pairs for h in range(2)]
        return lax.ppermute(value, ("tm", "head"), crossed)

    xp = over_head(inputs)
    b0 = over_b(inputs)
    b1 = over_b_and_head(inputs)
    a0 = over_a(inputs)
    *staged, pack = stage(w_query, w_key, w_value, w_out, inputs, cotangent, kernel)
    xp, a0, *staged = lax.optimization_barrier((xp, a0, *staged))
    w_query, w_key, w_value, w_out, inputs, cotangent, kernel = staged
    a1 = over_a(xp)
    q, k, v = call(
        own_kernel, (inputs, xp, w_query, w_key, w_value), (big, big, big), us=0.0
    )
    q, pack = lax.optimization_barrier((q, pack))
    pack_p = over_head(pack)
    edge = ((2 * EDGE, D), BF16)
    ka, va, kb, vb, probs, att, edges = call(
        attend_kernel,
        (a0, a1, b0, b1, w_key, w_value, w_out, q, k, v),
        (big, big, big, big, ((HEADS, ROWS, 3 * ROWS), BF16), big, edge),
        us=4.0,
    )
    edges_p = over_head(edges)
    (part,) = call(project_out_kernel, (att, w_out), (((ROWS, D), BF16),), us=1.0)
    part_p = over_head(part)
    to_a, to_b = call(
        merge_kernel, (edges, edges_p, cotangent, pack_p), (edge, edge), us=3.0
    )
    eb = over_b(to_b)
    ea = over_a(to_a)
    chunked = ((CHUNKS, EXT, LANES), F32)
    tall = ((ROWS, LANES), F32)
    output, dh, datt, gk = call(
        conv_kernel,
        (
            inputs, xp, a0, a1, b0, b1, part, part_p, ea, eb, cotangent, pack_p,
            kernel, w_out,
        ),
        (big, ((ROWS, SHARE), F32), big, ((KW, SHARE), F32)),
        scratch=(
            chunked, chunked, chunked, ((CHUNKS, ROWS, LANES), F32), ((ROWS, SHARE), F32),
            ((CHUNKS, 16, LANES), F32), tall, tall, tall, ((ROWS, D), BF16),
        ),
        us=5.0,
        mib=12,
    )
    chain = [gk]
    assert count == 128
    for steps in ((1,), (32, 64, 96), (8, 16, 24), (2, 4, 6)):
        last = chain[-1]
        parts = [
            lax.ppermute(last, "tm", [(i, i ^ step) for i in range(count)]) for step in steps
        ]
        chain.extend(call(sum_kernel, (last, *parts), (((KW, SHARE), F32),), us=0.2, mib=1))
    pair = ((2, ROWS, SHARE), BF16)
    dq_b, dkv_b = call(
        functools.partial(back_halo_kernel, which=2),
        (q, kb, vb, datt, att, probs),
        (((ROWS, SHARE), F32), pair),
        us=1.5,
    )
    got_b = over_b(dkv_b)
    dq_ab, dkv_a = call(
        functools.partial(back_halo_kernel, which=1),
        (q, ka, va, datt, att, probs, dq_b, chain[1]),
        (((ROWS, SHARE), F32), pair),
        us=1.5,
    )
    got_a = over_a(dkv_a)
    dkv, pin = call(
        back_own_kernel,
        (q, k, v, datt, att, probs, dq_ab, w_query, chain[1]),
        (((2, ROWS, SHARE), F32), ((ROWS, D), F32)),
        us=2.0,
    )
    send, keep, stat = call(
        project_kernel,
        (inputs, xp, dkv, got_a, got_b, pin, w_key, w_value, chain[2]),
        (((ROWS, SHARE + LANES), BF16), ((ROWS, SHARE), F32), tall),
        us=1.5,
    )
    got = over_head(send)
    (grad,) = call(
        final_kernel, (inputs, xp, keep, stat, got, dh, chain[3]), (big,), us=1.0
    )
    return output, grad, chain[-1]


def solution(mesh):
    placed = (
        P("tm", "head"),
        P(None, "head"),
        P(None, "head"),
        P(None, "head"),
        P("head", None),
        P(None, "head"),
        P("tm", "head"),
    )
    return jax.shard_map(
        local,
        mesh=mesh,
        in_specs=placed,
        out_specs=(P("tm", "head"), P("tm", "head"), P(None, "head")),
        check_vma=False,
    )
```

```python
import functools
import jax
import jax.numpy as jnp
from jax import lax
from jax.experimental import pallas as pl
from jax.experimental.pallas import tpu as pltpu
from jax.sharding import PartitionSpec as P

D = 1024
HEAD_DIM = 128
BLOCK = 128
CONTEXT = 2
KW = 9
EPSILON = 1e-05
MASKED = -1e30

ROWS = CONTEXT * BLOCK
SHARE = 512
HEADS = SHARE // HEAD_DIM
LANES = 128
EDGE = 16
RIM = 32
MID = ROWS - 2 * RIM
CHUNKS = D // LANES
HALF_CHUNKS = SHARE // LANES
PAD = 16
EXT = ROWS + 2 * PAD
HALF = KW // 2
SCALE = HEAD_DIM ** (-0.5)
F32 = jnp.float32
BF16 = jnp.bfloat16


def nn(a, b):
    return lax.dot_general(a, b, (((1,), (0,)), ((), ())), preferred_element_type=F32)


def nt(a, b):
    return lax.dot_general(a, b, (((1,), (1,)), ((), ())), preferred_element_type=F32)


def tn(a, b):
    return lax.dot_general(a, b, (((0,), (0,)), ((), ())), preferred_element_type=F32)


def row_sum(a):
    return jnp.sum(a, axis=1, keepdims=True)


def moments(a, b):
    center = (row_sum(a) + row_sum(b)) * (1.0 / D)
    spread = (row_sum(a * a) + row_sum(b * b)) * (1.0 / D) - center * center
    return center, lax.rsqrt(spread + EPSILON)


def norm_pair(a, b):
    a = a.astype(F32)
    b = b.astype(F32)
    center, rstd = moments(a, b)
    return (a - center) * rstd, (b - center) * rstd, rstd


def placement():
    place = lax.axis_index("tm")
    last = lax.axis_size("tm") - 1
    odd = lax.rem(place, 2)
    left = (place > 0).astype(jnp.int32)
    right = (place < last).astype(jnp.int32)
    return odd, left, right


def own_other():
    h = lax.axis_index("head")
    own = pl.ds(pl.multiple_of(h * SHARE, SHARE), SHARE)
    other = pl.ds(pl.multiple_of((1 - h) * SHARE, SHARE), SHARE)
    return own, other


def lanes_of(head):
    return slice(head * HEAD_DIM, (head + 1) * HEAD_DIM)


def band_bias(right, valid, rows):
    row = (lax.broadcasted_iota(jnp.int32, (rows, ROWS), 0) >= rows // 2).astype(jnp.int32)
    col = (lax.broadcasted_iota(jnp.int32, (rows, ROWS), 1) >= BLOCK).astype(jnp.int32)
    hidden = ((row - col) == 1 - 2 * right) | (valid == 0)
    return jnp.where(hidden, MASKED, 0.0).astype(F32)


def own_kernel(xo, xp, wq, wk, wv, q, k, v):
    own, other = own_other()
    no, np_, _ = norm_pair(xo[...], xp[...])
    no = no.astype(BF16)
    np_ = np_.astype(BF16)
    for w, out in ((wq, q), (wk, k), (wv, v)):
        out[...] = (nn(no, w[own, :]) + nn(np_, w[other, :])).astype(BF16)


def halo_kv(xo, xp, wk, wv, k, v):
    own, other = own_other()
    no, np_, _ = norm_pair(xo[...], xp[...])
    no = no.astype(BF16)
    np_ = np_.astype(BF16)
    for w, out in ((wk, k), (wv, v)):
        out[...] = (nn(no, w[own, :]) + nn(np_, w[other, :])).astype(BF16)


def attend(rows, q, k, v, ka, va, kb, vb, wo, p, att, part):
    odd, left, right = placement()
    height = att.shape[0]
    bias_a = band_bias(1 - odd, 1, height)
    bias_b = band_bias(odd, jnp.where(odd == 1, right, left), height)
    for head in range(HEADS):
        f = lanes_of(head)
        qh = jnp.concatenate([q[at, f] for at in rows], axis=0)
        scores = (
            nt(qh, k[:, f]) * SCALE,
            nt(qh, ka[:, f]) * SCALE + bias_a,
            nt(qh, kb[:, f]) * SCALE + bias_b,
        )
        top = functools.reduce(jnp.maximum, scores)
        top = jnp.max(top, axis=1, keepdims=True)
        scores = [jnp.exp(s - top) for s in scores]
        inverse = 1.0 / row_sum(sum(scores))
        out = 0.0
        for n, (s, values) in enumerate(zip(scores, (v, va, vb))):
            s = (s * inverse).astype(BF16)
            p[head, :, n * ROWS:(n + 1) * ROWS] = s
            out = out + nn(s, values[:, f])
        att[:, f] = out.astype(BF16)
    own, other = own_other()
    part[:, :SHARE] = nn(att[...], wo[:, own]).astype(BF16)
    part[:, SHARE:] = nn(att[...], wo[:, other]).astype(BF16)


def attend_rim_kernel(a0, a1, b0, b1, wk, wv, wo, q, k, v, ka, va, kb, vb, p, att, part):
    halo_kv(a0, a1, wk, wv, ka, va)
    halo_kv(b0, b1, wk, wv, kb, vb)
    rows = (slice(0, RIM), slice(ROWS - RIM, ROWS))
    attend(rows, q, k, v, ka, va, kb, vb, wo, p, att, part)


def attend_mid_kernel(wo, q, k, v, ka, va, kb, vb, p, att, part):
    attend((slice(RIM, ROWS - RIM),), q, k, v, ka, va, kb, vb, wo, p, att, part)


def in_order(rim, mid):
    return jnp.concatenate([rim[:RIM], mid, rim[RIM:]], axis=0)


def edge_rows(rows):
    odd, _, _ = placement()
    last = rows - EDGE
    return (
        pl.ds(pl.multiple_of((1 - odd) * last, EDGE), EDGE),
        pl.ds(pl.multiple_of(odd * last, EDGE), EDGE),
    )


def merge_kernel(part, part_p, co, cp, to_a, to_b):
    for at, at_c, out in zip(edge_rows(2 * RIM), edge_rows(ROWS), (to_a, to_b)):
        mine = part[at, :].astype(F32)
        theirs = part_p[at, :].astype(F32)
        out[:EDGE, :SHARE] = (mine[:, :SHARE] + theirs[:, SHARE:]).astype(BF16)
        out[:EDGE, SHARE:] = (mine[:, SHARE:] + theirs[:, :SHARE]).astype(BF16)
        out[EDGE:, :SHARE] = co[at_c, :]
        out[EDGE:, SHARE:] = cp[at_c, :]


def conv_kernel(
    xo, xp, a0, a1, b0, b1, rim, rim_p, mid, mid_p, ea, eb, co, cp, to, wo,
    output, dh, datt, gk,
    n2s, cs, dzs, dns, hs, taps, rs2, sum0, sum1, dhb,
):
    odd, left, right = placement()
    own, other = own_other()
    is_odd = odd == 1
    step = 32
    tp = unpack_taps(cp)
    for c in range(HALF_CHUNKS):
        f = slice(c * LANES, (c + 1) * LANES)
        taps[c, :KW, :] = to[:, f]
        taps[HALF_CHUNKS + c, :KW, :] = tp[:, f]

    def rows_in(index, carry, part, part_p, shift):
        r = pl.multiple_of(index * step, step)
        source = pl.ds(pl.multiple_of(r - shift, step), step)
        rows = pl.ds(r, step)
        held = pl.ds(pl.multiple_of(PAD + r, PAD), step)
        p = part[source, :].astype(F32)
        pp = part_p[source, :].astype(F32)
        ho = xo[rows, :].astype(F32) + p[:, :SHARE] + pp[:, SHARE:]
        hp = xp[rows, :].astype(F32) + p[:, SHARE:] + pp[:, :SHARE]
        center, rstd = moments(ho, hp)
        hs[rows, :] = ho
        rs2[rows, :] = jnp.broadcast_to(rstd, (step, LANES))
        ctan = co[rows, :].astype(F32)
        ctan_p = cp[rows, :].astype(F32)
        for c in range(HALF_CHUNKS):
            f = slice(c * LANES, (c + 1) * LANES)
            n2s[c, held, :] = (ho[:, f] - center) * rstd
            n2s[HALF_CHUNKS + c, held, :] = (hp[:, f] - center) * rstd
            cs[c, held, :] = ctan[:, f]
            cs[HALF_CHUNKS + c, held, :] = ctan_p[:, f]
        return carry

    for first, last, part, part_p, shift in (
        (0, RIM, rim, rim_p, 0),
        (RIM, ROWS - RIM, mid, mid_p, RIM),
        (ROWS - RIM, ROWS, rim, rim_p, MID),
    ):
        body = functools.partial(rows_in, part=part, part_p=part_p, shift=shift)
        lax.fori_loop(first // step, last // step, body, 0)

    pa = ea[:EDGE, :].astype(F32)
    pb = eb[:EDGE, :].astype(F32)
    sides = (
        (slice(ROWS - EDGE, ROWS), is_odd, 0, left),
        (slice(0, EDGE), jnp.logical_not(is_odd), PAD + ROWS, right),
    )
    for x_rows, from_a, at, valid in sides:
        def pick(one, two):
            return jnp.where(from_a, one.astype(F32), two.astype(F32))

        pe = pick(pa, pb)
        ho = pick(a0[x_rows, :], b0[x_rows, :]) + pe[:, :SHARE]
        hp = pick(a1[x_rows, :], b1[x_rows, :]) + pe[:, SHARE:]
        center, rstd = moments(ho, hp)
        ctan = pick(ea[EDGE:, :SHARE], eb[EDGE:, :SHARE])
        ctan_p = pick(ea[EDGE:, SHARE:], eb[EDGE:, SHARE:])
        inside = valid == 1
        for c in range(HALF_CHUNKS):
            f = slice(c * LANES, (c + 1) * LANES)
            for d, hh, cc in ((c, ho, ctan), (HALF_CHUNKS + c, hp, ctan_p)):
                n2s[d, at:at + EDGE, :] = jnp.where(inside, (hh[:, f] - center) * rstd, 0.0)
                cs[d, at:at + EDGE, :] = jnp.where(inside, cc[:, f], 0.0)

    piece = 136

    def forward(c, carry, mine):
        w = taps[c]
        for r0 in (8, 8 + piece):
            z = w[0:1, :] * n2s[c, r0 - HALF:r0 - HALF + piece, :]
            for tap in range(1, KW):
                at = r0 + tap - HALF
                z = z + w[tap:tap + 1, :] * n2s[c, at:at + piece, :]
            gate = jax.nn.sigmoid(z)
            dzs[c, r0:r0 + piece, :] = cs[c, r0:r0 + piece, :] * gate * (1.0 + z * (1.0 - gate))
            if mine:
                lo = max(r0, PAD)
                hi = min(r0 + piece, PAD + ROWS)
                lane = pl.ds(pl.multiple_of(c * LANES, LANES), LANES)
                mix = (z * gate)[lo - r0:hi - r0, :]
                hs[lo - PAD:hi - PAD, lane] = hs[lo - PAD:hi - PAD, lane] + mix
        if mine:
            lane = pl.ds(pl.multiple_of(c * LANES, LANES), LANES)
            dz = dzs[c, PAD:PAD + ROWS, :]
            for tap in range(KW):
                at = PAD + tap - HALF
                gk[tap:tap + 1, lane] = jnp.sum(
                    dz * n2s[c, at:at + ROWS, :], axis=0, keepdims=True
                )
        return carry

    lax.fori_loop(0, HALF_CHUNKS, functools.partial(forward, mine=True), 0)
    lax.fori_loop(HALF_CHUNKS, CHUNKS, functools.partial(forward, mine=False), 0)
    output[...] = hs[...].astype(BF16)

    sum0[...] = jnp.zeros_like(sum0)
    sum1[...] = jnp.zeros_like(sum1)

    def backward(c, carry):
        w = taps[c]
        for r0 in (0, ROWS // 2):
            at = PAD + r0 + HALF
            g = w[0:1, :] * dzs[c, at:at + ROWS // 2, :]
            for tap in range(1, KW):
                at = PAD + r0 + HALF - tap
                g = g + w[tap:tap + 1, :] * dzs[c, at:at + ROWS // 2, :]
            dns[c, r0:r0 + ROWS // 2, :] = g
            half = slice(r0, r0 + ROWS // 2)
            sum0[half, :] = sum0[half, :] + g
            sum1[half, :] = sum1[half, :] + g * n2s[c, PAD + r0:PAD + r0 + ROWS // 2, :]
        return carry

    lax.fori_loop(0, CHUNKS, backward, 0)
    sum0[...] = jnp.broadcast_to(row_sum(sum0[...]) * (1.0 / D), (ROWS, LANES))
    sum1[...] = jnp.broadcast_to(row_sum(sum1[...]) * (1.0 / D), (ROWS, LANES))

    def finish(c, carry, mine):
        lane = pl.ds(pl.multiple_of(c * LANES, LANES), LANES)
        value = cs[c, PAD:PAD + ROWS, :] + rs2[...] * (
            dns[c] - sum0[...] - n2s[c, PAD:PAD + ROWS, :] * sum1[...]
        )
        if mine:
            dh[:, lane] = value
        dhb[:, lane] = value.astype(BF16)
        return carry

    lax.fori_loop(0, HALF_CHUNKS, functools.partial(finish, mine=True), 0)
    lax.fori_loop(HALF_CHUNKS, CHUNKS, functools.partial(finish, mine=False), 0)
    datt[...] = (nt(dhb[:, :SHARE], wo[:, own]) + nt(dhb[:, SHARE:], wo[:, other])).astype(BF16)


def pair_grad(qh, kh, vh, gh, p, delta):
    dots = nt(gh, vh)
    ds = (p.astype(F32) * (dots - delta) * SCALE).astype(BF16)
    return nn(ds, kh), tn(ds, qh), tn(p, gh)


def back_halo_kernel(q, k, v, datt, att, att_mid, p, p_mid, *refs, which):
    dq, dkv = refs[-2:]
    at = slice(which * ROWS, (which + 1) * ROWS)
    for head in range(HEADS):
        f = lanes_of(head)
        gh = datt[:, f]
        delta = row_sum(gh.astype(F32) * in_order(att[:, f], att_mid[:, f]).astype(F32))
        probs = in_order(p[head, :, at], p_mid[head, :, at])
        d_q, d_k, d_v = pair_grad(q[:, f], k[:, f], v[:, f], gh, probs, delta)
        dq[:, f] = d_q + refs[0][:, f] if which == 1 else d_q
        dkv[0, :, f] = d_k.astype(BF16)
        dkv[1, :, f] = d_v.astype(BF16)


def back_own_kernel(q, k, v, datt, att, att_mid, p, p_mid, dq_ab, wq, after, dkv, pin):
    dq = []
    for head in range(HEADS):
        f = lanes_of(head)
        gh = datt[:, f]
        delta = row_sum(gh.astype(F32) * in_order(att[:, f], att_mid[:, f]).astype(F32))
        probs = in_order(p[head, :, :ROWS], p_mid[head, :, :ROWS])
        d_q, d_k, d_v = pair_grad(q[:, f], k[:, f], v[:, f], gh, probs, delta)
        dkv[0, :, f] = d_k
        dkv[1, :, f] = d_v
        dq.append((d_q + dq_ab[:, f]).astype(BF16))
    own, other = own_other()
    dq = jnp.concatenate(dq, axis=1)
    pin[:, :SHARE] = nt(dq, wq[own, :])
    pin[:, SHARE:] = nt(dq, wq[other, :])


def project_kernel(xo, xp, dkv, got_a, got_b, pin, wk, wv, after, send, keep, stat):
    own, other = own_other()
    dk = (dkv[0] + got_a[0].astype(F32) + got_b[0].astype(F32)).astype(BF16)
    dv = (dkv[1] + got_a[1].astype(F32) + got_b[1].astype(F32)).astype(BF16)
    p_own = pin[:, :SHARE] + nt(dk, wk[own, :]) + nt(dv, wv[own, :])
    p_other = pin[:, SHARE:] + nt(dk, wk[other, :]) + nt(dv, wv[other, :])
    no, np_, _ = norm_pair(xo[...], xp[...])
    s0 = row_sum(p_own) + row_sum(p_other)
    s1 = row_sum(p_own * no) + row_sum(p_other * np_)
    keep[...] = p_own
    send[:, :SHARE] = p_other.astype(BF16)
    lane = lax.broadcasted_iota(jnp.int32, (ROWS, LANES), 1)
    s0_hi = s0.astype(BF16).astype(F32)
    s1_hi = s1.astype(BF16).astype(F32)
    packed = jnp.where(lane == 0, s0_hi, 0.0)
    packed = jnp.where(lane == 1, s0 - s0_hi, packed)
    packed = jnp.where(lane == 2, s1_hi, packed)
    packed = jnp.where(lane == 3, s1 - s1_hi, packed)
    send[:, SHARE:] = packed.astype(BF16)
    stat[...] = jnp.where(lane == 0, s0, jnp.where(lane == 2, s1, 0.0))


def final_kernel(xo, xp, keep, stat, got, dh, after, grad):
    no, _, rstd = norm_pair(xo[...], xp[...])
    dn1 = keep[...] + got[:, :SHARE].astype(F32)
    lane = lax.broadcasted_iota(jnp.int32, (ROWS, LANES), 1)
    sums = stat[...] + got[:, SHARE:].astype(F32)
    s0 = row_sum(jnp.where(lane < 2, sums, 0.0)) * (1.0 / D)
    s1 = row_sum(jnp.where(lane < 2, 0.0, sums)) * (1.0 / D)
    grad[...] = (dh[...] + rstd * (dn1 - s0 - no * s1)).astype(BF16)


def sum_kernel(*refs):
    refs[-1][...] = sum(ref[...] for ref in refs[:-1])


def stage_kernel(*refs):
    half = (len(refs) - 2) // 2
    pack, sems = refs[-2:]
    copies = [
        pltpu.make_async_copy(refs[i], refs[half + i], sems.at[i]) for i in range(half)
    ]
    for copy in copies:
        copy.start()
    for copy in copies:
        copy.wait()
    co, taps = refs[2 * half - 2:2 * half]
    pack[:ROWS, :] = co[...]
    rest = taps[...]
    for n in range(3):
        piece = rest.astype(BF16)
        pack[ROWS + n * EDGE:ROWS + n * EDGE + KW, :] = piece
        rest = rest - piece.astype(F32)


def unpack_taps(pack):
    return sum(
        pack[ROWS + n * EDGE:ROWS + n * EDGE + KW, :].astype(F32) for n in (2, 1, 0)
    )


def stage(*arrays):
    outs = [pltpu.VMEM(a.shape, a.dtype) for a in arrays]
    outs.append(pltpu.VMEM((ROWS + 3 * EDGE, SHARE), BF16))
    return pl.pallas_call(
        stage_kernel,
        out_shape=outs,
        in_specs=[pl.BlockSpec(memory_space=pltpu.HBM)] * len(arrays),
        out_specs=[pl.BlockSpec(memory_space=pltpu.VMEM)] * len(outs),
        scratch_shapes=[pltpu.SemaphoreType.DMA((len(arrays),))],
        compiler_params=pltpu.CompilerParams(vmem_limit_bytes=6 * 1024 * 1024),
        cost_estimate=pl.CostEstimate(flops=0, bytes_accessed=64 * 1024 * 1024, transcendentals=0),
    )(*[pltpu.with_memory_space_constraint(a, pltpu.HBM) for a in arrays])


def call(kernel, args, outs, scratch=(), us=1.0, mib=6):
    whole = pl.BlockSpec(memory_space=pltpu.VMEM)
    return pl.pallas_call(
        kernel,
        out_shape=[jax.ShapeDtypeStruct(shape, dtype) for shape, dtype in outs],
        in_specs=[whole] * len(args),
        out_specs=[whole] * len(outs),
        scratch_shapes=[pltpu.VMEM(shape, dtype) for shape, dtype in scratch],
        compiler_params=pltpu.CompilerParams(vmem_limit_bytes=mib * 1024 * 1024),
        cost_estimate=pl.CostEstimate(
            flops=int(us * 1e10), bytes_accessed=int(us * 1e7), transcendentals=0
        ),
    )(*args)


def local(inputs, w_query, w_key, w_value, w_out, kernel, cotangent):
    count = lax.axis_size("tm")
    assert inputs.shape == (ROWS, SHARE) and count % 2 == 0
    def over_head(value):
        return lax.ppermute(value, "head", [(0, 1), (1, 0)])

    def over_a(value):
        return lax.ppermute(value, "tm", [(i, i ^ 1) for i in range(count)])

    def over_b(value):
        pairs = [(i, i + 1) for i in range(1, count - 1, 2)]
        return lax.ppermute(value, "tm", pairs + [(j, i) for i, j in pairs])

    big = ((ROWS, SHARE), BF16)
    def over_b_and_head(value):
        pairs = [(i, i + 1) for i in range(1, count - 1, 2)]
        pairs = pairs + [(j, i) for i, j in pairs]
        crossed = [(2 * i + h, 2 * j + 1 - h) for i, j in pairs for h in range(2)]
        return lax.ppermute(value, ("tm", "head"), crossed)

    xp = over_head(inputs)
    b0 = over_b(inputs)
    b1 = over_b_and_head(inputs)
    a0 = over_a(inputs)
    *staged, pack = stage(w_query, w_key, w_value, w_out, inputs, cotangent, kernel)
    xp, a0, *staged = lax.optimization_barrier((xp, a0, *staged))
    w_query, w_key, w_value, w_out, inputs, cotangent, kernel = staged
    a1 = over_a(xp)
    q, k, v = call(
        own_kernel, (inputs, xp, w_query, w_key, w_value), (big, big, big), us=0.0
    )
    q, pack = lax.optimization_barrier((q, pack))
    pack_p = over_head(pack)
    edge = ((2 * EDGE, D), BF16)
    chunk = [
        (((HEADS, rows, 3 * ROWS), BF16), ((rows, SHARE), BF16), ((rows, D), BF16))
        for rows in (2 * RIM, MID)
    ]
    ka, va, kb, vb, p_rim, att_rim, rim = call(
        attend_rim_kernel,
        (a0, a1, b0, b1, w_key, w_value, w_out, q, k, v),
        (big, big, big, big, *chunk[0]),
        us=2.0,
    )
    rim_p = over_head(rim)
    p_mid, att_mid, mid = call(
        attend_mid_kernel, (w_out, q, k, v, ka, va, kb, vb), chunk[1], us=2.0
    )
    mid_p = over_head(mid)
    attended = (att_rim, att_mid, p_rim, p_mid)
    to_a, to_b = call(
        merge_kernel, (rim, rim_p, cotangent, pack_p), (edge, edge), us=3.0
    )
    eb = over_b(to_b)
    ea = over_a(to_a)
    chunked = ((CHUNKS, EXT, LANES), F32)
    tall = ((ROWS, LANES), F32)
    output, dh, datt, gk = call(
        conv_kernel,
        (
            inputs, xp, a0, a1, b0, b1, rim, rim_p, mid, mid_p, ea, eb, cotangent, pack_p,
            kernel, w_out,
        ),
        (big, ((ROWS, SHARE), F32), big, ((KW, SHARE), F32)),
        scratch=(
            chunked, chunked, chunked, ((CHUNKS, ROWS, LANES), F32), ((ROWS, SHARE), F32),
            ((CHUNKS, 16, LANES), F32), tall, tall, tall, ((ROWS, D), BF16),
        ),
        us=5.0,
        mib=12,
    )
    chain = [gk]
    assert count == 128
    for steps in ((1,), (32, 64, 96), (8, 16, 24), (2, 4, 6)):
        last = chain[-1]
        parts = [
            lax.ppermute(last, "tm", [(i, i ^ step) for i in range(count)]) for step in steps
        ]
        chain.extend(call(sum_kernel, (last, *parts), (((KW, SHARE), F32),), us=0.2, mib=1))
    pair = ((2, ROWS, SHARE), BF16)
    dq_b, dkv_b = call(
        functools.partial(back_halo_kernel, which=2),
        (q, kb, vb, datt, *attended),
        (((ROWS, SHARE), F32), pair),
        us=1.5,
    )
    got_b = over_b(dkv_b)
    dq_ab, dkv_a = call(
        functools.partial(back_halo_kernel, which=1),
        (q, ka, va, datt, *attended, dq_b, chain[1]),
        (((ROWS, SHARE), F32), pair),
        us=1.5,
    )
    got_a = over_a(dkv_a)
    dkv, pin = call(
        back_own_kernel,
        (q, k, v, datt, *attended, dq_ab, w_query, chain[1]),
        (((2, ROWS, SHARE), F32), ((ROWS, D), F32)),
        us=2.0,
    )
    send, keep, stat = call(
        project_kernel,
        (inputs, xp, dkv, got_a, got_b, pin, w_key, w_value, chain[2]),
        (((ROWS, SHARE + LANES), BF16), ((ROWS, SHARE), F32), tall),
        us=1.5,
    )
    got = over_head(send)
    (grad,) = call(
        final_kernel, (inputs, xp, keep, stat, got, dh, chain[3]), (big,), us=1.0
    )
    return output, grad, chain[-1]


def solution(mesh):
    placed = (
        P("tm", "head"),
        P(None, "head"),
        P(None, "head"),
        P(None, "head"),
        P("head", None),
        P(None, "head"),
        P("tm", "head"),
    )
    return jax.shard_map(
        local,
        mesh=mesh,
        in_specs=placed,
        out_specs=(P("tm", "head"), P("tm", "head"), P(None, "head")),
        check_vma=False,
    )
```

```python
import functools
import jax
import jax.numpy as jnp
from jax import lax
from jax.experimental import pallas as pl
from jax.experimental.pallas import tpu as pltpu
from jax.sharding import PartitionSpec as P

D = 1024
HEAD_DIM = 128
BLOCK = 128
CONTEXT = 2
KW = 9
EPSILON = 1e-05
MASKED = -1e30

ROWS = CONTEXT * BLOCK
SHARE = 512
HEADS = SHARE // HEAD_DIM
LANES = 128
EDGE = 16
RIM = 32
MID = ROWS - 2 * RIM
CHUNKS = D // LANES
HALF_CHUNKS = SHARE // LANES
PAD = 16
EXT = ROWS + 2 * PAD
HALF = KW // 2
SCALE = HEAD_DIM ** (-0.5)
F32 = jnp.float32
BF16 = jnp.bfloat16


def nn(a, b):
    return lax.dot_general(a, b, (((1,), (0,)), ((), ())), preferred_element_type=F32)


def nt(a, b):
    return lax.dot_general(a, b, (((1,), (1,)), ((), ())), preferred_element_type=F32)


def tn(a, b):
    return lax.dot_general(a, b, (((0,), (0,)), ((), ())), preferred_element_type=F32)


def row_sum(a):
    return jnp.sum(a, axis=1, keepdims=True)


def moments(a, b):
    center = (row_sum(a) + row_sum(b)) * (1.0 / D)
    spread = (row_sum(a * a) + row_sum(b * b)) * (1.0 / D) - center * center
    return center, lax.rsqrt(spread + EPSILON)


def norm_pair(a, b):
    a = a.astype(F32)
    b = b.astype(F32)
    center, rstd = moments(a, b)
    return (a - center) * rstd, (b - center) * rstd, rstd


def placement():
    place = lax.axis_index("tm")
    last = lax.axis_size("tm") - 1
    odd = lax.rem(place, 2)
    left = (place > 0).astype(jnp.int32)
    right = (place < last).astype(jnp.int32)
    return odd, left, right


def own_other():
    h = lax.axis_index("head")
    own = pl.ds(pl.multiple_of(h * SHARE, SHARE), SHARE)
    other = pl.ds(pl.multiple_of((1 - h) * SHARE, SHARE), SHARE)
    return own, other


def lanes_of(head):
    return slice(head * HEAD_DIM, (head + 1) * HEAD_DIM)


def band_bias(right, valid, rows):
    row = (lax.broadcasted_iota(jnp.int32, (rows, ROWS), 0) >= rows // 2).astype(jnp.int32)
    col = (lax.broadcasted_iota(jnp.int32, (rows, ROWS), 1) >= BLOCK).astype(jnp.int32)
    hidden = ((row - col) == 1 - 2 * right) | (valid == 0)
    return jnp.where(hidden, MASKED, 0.0).astype(F32)


def own_kernel(xo, xp, wq, wk, wv, q, k, v):
    own, other = own_other()
    no, np_, _ = norm_pair(xo[...], xp[...])
    no = no.astype(BF16)
    np_ = np_.astype(BF16)
    for w, out in ((wq, q), (wk, k), (wv, v)):
        out[...] = (nn(no, w[own, :]) + nn(np_, w[other, :])).astype(BF16)


def halo_kv(xo, xp, wk, wv, k, v):
    own, other = own_other()
    no, np_, _ = norm_pair(xo[...], xp[...])
    no = no.astype(BF16)
    np_ = np_.astype(BF16)
    for w, out in ((wk, k), (wv, v)):
        out[...] = (nn(no, w[own, :]) + nn(np_, w[other, :])).astype(BF16)


def attend(rows, q, k, v, ka, va, kb, vb, wo, p, att, part):
    odd, left, right = placement()
    height = att.shape[0]
    bias_a = band_bias(1 - odd, 1, height)
    bias_b = band_bias(odd, jnp.where(odd == 1, right, left), height)
    for head in range(HEADS):
        f = lanes_of(head)
        qh = jnp.concatenate([q[at, f] for at in rows], axis=0)
        scores = (
            nt(qh, k[:, f]) * SCALE,
            nt(qh, ka[:, f]) * SCALE + bias_a,
            nt(qh, kb[:, f]) * SCALE + bias_b,
        )
        top = functools.reduce(jnp.maximum, scores)
        top = jnp.max(top, axis=1, keepdims=True)
        scores = [jnp.exp(s - top) for s in scores]
        inverse = 1.0 / row_sum(sum(scores))
        out = 0.0
        for n, (s, values) in enumerate(zip(scores, (v, va, vb))):
            s = (s * inverse).astype(BF16)
            p[head, :, n * ROWS:(n + 1) * ROWS] = s
            out = out + nn(s, values[:, f])
        att[:, f] = out.astype(BF16)
    own, other = own_other()
    part[:, :SHARE] = nn(att[...], wo[:, own]).astype(BF16)
    part[:, SHARE:] = nn(att[...], wo[:, other]).astype(BF16)


def attend_rim_kernel(b0, b1, wk, wv, wo, q, k, v, ka, va, kb, vb, p, att, part):
    halo_kv(b0, b1, wk, wv, kb, vb)
    rows = (slice(0, RIM), slice(ROWS - RIM, ROWS))
    attend(rows, q, k, v, ka, va, kb, vb, wo, p, att, part)


def attend_mid_kernel(wo, q, k, v, ka, va, kb, vb, p, att, part):
    attend((slice(RIM, ROWS - RIM),), q, k, v, ka, va, kb, vb, wo, p, att, part)


def in_order(rim, mid):
    return jnp.concatenate([rim[:RIM], mid, rim[RIM:]], axis=0)


def edge_rows(rows):
    odd, _, _ = placement()
    last = rows - EDGE
    return (
        pl.ds(pl.multiple_of((1 - odd) * last, EDGE), EDGE),
        pl.ds(pl.multiple_of(odd * last, EDGE), EDGE),
    )


def merge_kernel(part, part_p, co, cp, xo, xp, to_a, to_b):
    for at, at_c, out in zip(edge_rows(2 * RIM), edge_rows(ROWS), (to_a, to_b)):
        mine = part[at, :].astype(F32)
        theirs = part_p[at, :].astype(F32)
        out[:EDGE, :SHARE] = (mine[:, :SHARE] + theirs[:, SHARE:]).astype(BF16)
        out[:EDGE, SHARE:] = (mine[:, SHARE:] + theirs[:, :SHARE]).astype(BF16)
        out[EDGE:2 * EDGE, :SHARE] = co[at_c, :]
        out[EDGE:2 * EDGE, SHARE:] = cp[at_c, :]
        out[2 * EDGE:, :SHARE] = xo[at_c, :]
        out[2 * EDGE:, SHARE:] = xp[at_c, :]


def prepare_kernel(xo, xp, co, cp, no, np_, rstd, cs):
    no[...], np_[...], scale = norm_pair(xo[...], xp[...])
    rstd[...] = jnp.broadcast_to(scale, (ROWS, LANES))
    for c in range(HALF_CHUNKS):
        f = slice(c * LANES, (c + 1) * LANES)
        cs[c] = co[:, f].astype(F32)
        cs[HALF_CHUNKS + c] = cp[:ROWS, f].astype(F32)


def conv_kernel(
    xo, xp, rim, rim_p, mid, mid_p, ea, eb, cs, cp, to, wo,
    output, dh, datt, gk,
    n2s, ends, dzs, dns, hs, taps, rs2, sum0, sum1, dhb,
):
    odd, left, right = placement()
    own, other = own_other()
    is_odd = odd == 1
    step = 32
    tp = unpack_taps(cp)
    for c in range(HALF_CHUNKS):
        f = slice(c * LANES, (c + 1) * LANES)
        taps[c, :KW, :] = to[:, f]
        taps[HALF_CHUNKS + c, :KW, :] = tp[:, f]

    def rows_in(index, carry, part, part_p, shift):
        r = pl.multiple_of(index * step, step)
        source = pl.ds(pl.multiple_of(r - shift, step), step)
        rows = pl.ds(r, step)
        held = pl.ds(pl.multiple_of(PAD + r, PAD), step)
        p = part[source, :].astype(F32)
        pp = part_p[source, :].astype(F32)
        ho = xo[rows, :].astype(F32) + p[:, :SHARE] + pp[:, SHARE:]
        hp = xp[rows, :].astype(F32) + p[:, SHARE:] + pp[:, :SHARE]
        center, rstd = moments(ho, hp)
        hs[rows, :] = ho
        rs2[rows, :] = jnp.broadcast_to(rstd, (step, LANES))
        for c in range(HALF_CHUNKS):
            f = slice(c * LANES, (c + 1) * LANES)
            n2s[c, held, :] = (ho[:, f] - center) * rstd
            n2s[HALF_CHUNKS + c, held, :] = (hp[:, f] - center) * rstd
        return carry

    for first, last, part, part_p, shift in (
        (0, RIM, rim, rim_p, 0),
        (RIM, ROWS - RIM, mid, mid_p, RIM),
        (ROWS - RIM, ROWS, rim, rim_p, MID),
    ):
        body = functools.partial(rows_in, part=part, part_p=part_p, shift=shift)
        lax.fori_loop(first // step, last // step, body, 0, unroll=True)

    pa = ea[:EDGE, :].astype(F32)
    pb = eb[:EDGE, :].astype(F32)
    sides = (
        (is_odd, 0, 0, left),
        (jnp.logical_not(is_odd), PAD + ROWS, EDGE, right),
    )
    for from_a, at, end, valid in sides:
        def pick(one, two):
            return jnp.where(from_a, one.astype(F32), two.astype(F32))

        pe = pick(pa, pb)
        ho = pick(ea[2 * EDGE:, :SHARE], eb[2 * EDGE:, :SHARE]) + pe[:, :SHARE]
        hp = pick(ea[2 * EDGE:, SHARE:], eb[2 * EDGE:, SHARE:]) + pe[:, SHARE:]
        center, rstd = moments(ho, hp)
        ctan = pick(ea[EDGE:2 * EDGE, :SHARE], eb[EDGE:2 * EDGE, :SHARE])
        ctan_p = pick(ea[EDGE:2 * EDGE, SHARE:], eb[EDGE:2 * EDGE, SHARE:])
        inside = valid == 1
        for c in range(HALF_CHUNKS):
            f = slice(c * LANES, (c + 1) * LANES)
            for d, hh, cc in ((c, ho, ctan), (HALF_CHUNKS + c, hp, ctan_p)):
                n2s[d, at:at + EDGE, :] = jnp.where(inside, (hh[:, f] - center) * rstd, 0.0)
                ends[d, end:end + EDGE, :] = jnp.where(inside, cc[:, f], 0.0)

    piece = 136

    def forward(c, carry, mine):
        w = taps[c]
        for r0 in (8, 8 + piece):
            z = w[0:1, :] * n2s[c, r0 - HALF:r0 - HALF + piece, :]
            for tap in range(1, KW):
                at = r0 + tap - HALF
                z = z + w[tap:tap + 1, :] * n2s[c, at:at + piece, :]
            gate = jax.nn.sigmoid(z)
            if r0 < PAD:
                ctan = jnp.concatenate([ends[c, r0:PAD, :], cs[c, :r0 + piece - PAD, :]], axis=0)
            else:
                ctan = jnp.concatenate([cs[c, r0 - PAD:, :], ends[c, EDGE:PAD + 8, :]], axis=0)
            dzs[c, r0:r0 + piece, :] = ctan * gate * (1.0 + z * (1.0 - gate))
            if mine:
                lo = max(r0, PAD)
                hi = min(r0 + piece, PAD + ROWS)
                lane = pl.ds(pl.multiple_of(c * LANES, LANES), LANES)
                mix = (z * gate)[lo - r0:hi - r0, :]
                output[lo - PAD:hi - PAD, lane] = (hs[lo - PAD:hi - PAD, lane] + mix).astype(BF16)
        return carry

    lax.fori_loop(0, HALF_CHUNKS, functools.partial(forward, mine=True), 0, unroll=2)
    lax.fori_loop(HALF_CHUNKS, CHUNKS, functools.partial(forward, mine=False), 0, unroll=2)

    sum0[...] = jnp.zeros_like(sum0)
    sum1[...] = jnp.zeros_like(sum1)

    def backward(c, carry, mine):
        w = taps[c]
        for r0 in (0, ROWS // 2):
            half = slice(r0, r0 + ROWS // 2)
            n2 = n2s[c, PAD + r0:PAD + r0 + ROWS // 2, :]
            g = 0.0
            for tap in range(KW):
                at = PAD + r0 + HALF - tap
                dz = dzs[c, at:at + ROWS // 2, :]
                g = g + w[tap:tap + 1, :] * dz
                if mine:
                    lane = pl.ds(pl.multiple_of(c * LANES, LANES), LANES)
                    part = jnp.sum(dz * n2, axis=0, keepdims=True)
                    gk[tap:tap + 1, lane] = part if r0 == 0 else gk[tap:tap + 1, lane] + part
            dns[c, half, :] = g
            sum0[half, :] = sum0[half, :] + g
            sum1[half, :] = sum1[half, :] + g * n2
        return carry

    lax.fori_loop(0, HALF_CHUNKS, functools.partial(backward, mine=True), 0, unroll=2)
    lax.fori_loop(HALF_CHUNKS, CHUNKS, functools.partial(backward, mine=False), 0, unroll=2)
    sum0[...] = jnp.broadcast_to(row_sum(sum0[...]) * (1.0 / D), (ROWS, LANES))
    sum1[...] = jnp.broadcast_to(row_sum(sum1[...]) * (1.0 / D), (ROWS, LANES))

    def finish(c, carry, mine):
        lane = pl.ds(pl.multiple_of(c * LANES, LANES), LANES)
        value = cs[c] + rs2[...] * (
            dns[c] - sum0[...] - n2s[c, PAD:PAD + ROWS, :] * sum1[...]
        )
        if mine:
            dh[:, lane] = value
        dhb[:, lane] = value.astype(BF16)
        return carry

    lax.fori_loop(0, HALF_CHUNKS, functools.partial(finish, mine=True), 0, unroll=True)
    lax.fori_loop(HALF_CHUNKS, CHUNKS, functools.partial(finish, mine=False), 0, unroll=True)
    datt[...] = (nt(dhb[:, :SHARE], wo[:, own]) + nt(dhb[:, SHARE:], wo[:, other])).astype(BF16)


def pair_grad(qh, kh, vh, gh, p, delta):
    dots = nt(gh, vh)
    ds = (p.astype(F32) * (dots - delta) * SCALE).astype(BF16)
    return nn(ds, kh), tn(ds, qh), tn(p, gh)


def back_halo_kernel(q, k, v, datt, att, att_mid, p, p_mid, *refs, which):
    dq, dkv = refs[-2:]
    at = slice(which * ROWS, (which + 1) * ROWS)
    for head in range(HEADS):
        f = lanes_of(head)
        gh = datt[:, f]
        delta = row_sum(gh.astype(F32) * in_order(att[:, f], att_mid[:, f]).astype(F32))
        probs = in_order(p[head, :, at], p_mid[head, :, at])
        d_q, d_k, d_v = pair_grad(q[:, f], k[:, f], v[:, f], gh, probs, delta)
        dq[:, f] = d_q + refs[0][:, f] if which == 1 else d_q
        dkv[0, :, f] = d_k.astype(BF16)
        dkv[1, :, f] = d_v.astype(BF16)


def back_own_kernel(q, k, v, datt, att, att_mid, p, p_mid, dq_ab, wq, after, dkv, pin):
    dq = []
    for head in range(HEADS):
        f = lanes_of(head)
        gh = datt[:, f]
        delta = row_sum(gh.astype(F32) * in_order(att[:, f], att_mid[:, f]).astype(F32))
        probs = in_order(p[head, :, :ROWS], p_mid[head, :, :ROWS])
        d_q, d_k, d_v = pair_grad(q[:, f], k[:, f], v[:, f], gh, probs, delta)
        dkv[0, :, f] = d_k
        dkv[1, :, f] = d_v
        dq.append((d_q + dq_ab[:, f]).astype(BF16))
    own, other = own_other()
    dq = jnp.concatenate(dq, axis=1)
    pin[:, :SHARE] = nt(dq, wq[own, :])
    pin[:, SHARE:] = nt(dq, wq[other, :])


def project_kernel(n1o, n1p, dkv, got_a, got_b, pin, wk, wv, after, send, keep, stat):
    own, other = own_other()
    dk = (dkv[0] + got_a[0].astype(F32) + got_b[0].astype(F32)).astype(BF16)
    dv = (dkv[1] + got_a[1].astype(F32) + got_b[1].astype(F32)).astype(BF16)
    p_own = pin[:, :SHARE] + nt(dk, wk[own, :]) + nt(dv, wv[own, :])
    p_other = pin[:, SHARE:] + nt(dk, wk[other, :]) + nt(dv, wv[other, :])
    s0 = row_sum(p_own) + row_sum(p_other)
    s1 = row_sum(p_own * n1o[...]) + row_sum(p_other * n1p[...])
    keep[...] = p_own
    send[:, :SHARE] = p_other.astype(BF16)
    lane = lax.broadcasted_iota(jnp.int32, (ROWS, LANES), 1)
    s0_hi = s0.astype(BF16).astype(F32)
    s1_hi = s1.astype(BF16).astype(F32)
    packed = jnp.where(lane == 0, s0_hi, 0.0)
    packed = jnp.where(lane == 1, s0 - s0_hi, packed)
    packed = jnp.where(lane == 2, s1_hi, packed)
    packed = jnp.where(lane == 3, s1 - s1_hi, packed)
    send[:, SHARE:] = packed.astype(BF16)
    stat[...] = jnp.where(lane == 0, s0, jnp.where(lane == 2, s1, 0.0))


def final_kernel(n1o, rstd, keep, stat, got, dh, row, one, two, three, grad, taps):
    taps[...] = (row[...] + one[...]) + (two[...] + three[...])
    dn1 = keep[...] + got[:, :SHARE].astype(F32)
    lane = lax.broadcasted_iota(jnp.int32, (ROWS, LANES), 1)
    sums = stat[...] + got[:, SHARE:].astype(F32)
    s0 = row_sum(jnp.where(lane < 2, sums, 0.0)) * (1.0 / D)
    s1 = row_sum(jnp.where(lane < 2, 0.0, sums)) * (1.0 / D)
    grad[...] = (dh[...] + rstd[:, :1] * (dn1 - s0 - n1o[...] * s1)).astype(BF16)


def sum_kernel(*refs):
    refs[-1][...] = sum(ref[...] for ref in refs[:-1])


def stage_kernel(*refs):
    half = (len(refs) - 2) // 2
    pack, sems = refs[-2:]
    copies = [
        pltpu.make_async_copy(refs[i], refs[half + i], sems.at[i]) for i in range(half)
    ]
    for copy in copies:
        copy.start()
    for copy in copies:
        copy.wait()
    co, taps = refs[2 * half - 2:2 * half]
    pack[:ROWS, :] = co[...]
    rest = taps[...]
    for n in range(3):
        piece = rest.astype(BF16)
        pack[ROWS + n * EDGE:ROWS + n * EDGE + KW, :] = piece
        rest = rest - piece.astype(F32)


def unpack_taps(pack):
    return sum(
        pack[ROWS + n * EDGE:ROWS + n * EDGE + KW, :].astype(F32) for n in (2, 1, 0)
    )


def stage(*arrays):
    outs = [pltpu.VMEM(a.shape, a.dtype) for a in arrays]
    outs.append(pltpu.VMEM((ROWS + 3 * EDGE, SHARE), BF16))
    return pl.pallas_call(
        stage_kernel,
        out_shape=outs,
        in_specs=[pl.BlockSpec(memory_space=pltpu.HBM)] * len(arrays),
        out_specs=[pl.BlockSpec(memory_space=pltpu.VMEM)] * len(outs),
        scratch_shapes=[pltpu.SemaphoreType.DMA((len(arrays),))],
        compiler_params=pltpu.CompilerParams(vmem_limit_bytes=6 * 1024 * 1024),
        cost_estimate=pl.CostEstimate(flops=0, bytes_accessed=64 * 1024 * 1024, transcendentals=0),
    )(*[pltpu.with_memory_space_constraint(a, pltpu.HBM) for a in arrays])


def call(kernel, args, outs, scratch=(), us=1.0, mib=6):
    whole = pl.BlockSpec(memory_space=pltpu.VMEM)
    return pl.pallas_call(
        kernel,
        out_shape=[jax.ShapeDtypeStruct(shape, dtype) for shape, dtype in outs],
        in_specs=[whole] * len(args),
        out_specs=[whole] * len(outs),
        scratch_shapes=[pltpu.VMEM(shape, dtype) for shape, dtype in scratch],
        compiler_params=pltpu.CompilerParams(vmem_limit_bytes=mib * 1024 * 1024),
        cost_estimate=pl.CostEstimate(
            flops=int(us * 1e10), bytes_accessed=int(us * 1e7), transcendentals=0
        ),
    )(*args)


def local(inputs, w_query, w_key, w_value, w_out, kernel, cotangent):
    count = lax.axis_size("tm")
    assert inputs.shape == (ROWS, SHARE) and count % 2 == 0
    def over_head(value):
        return lax.ppermute(value, "head", [(0, 1), (1, 0)])

    def over_a(value):
        return lax.ppermute(value, "tm", [(i, i ^ 1) for i in range(count)])

    def over_b(value):
        pairs = [(i, i + 1) for i in range(1, count - 1, 2)]
        return lax.ppermute(value, "tm", pairs + [(j, i) for i, j in pairs])

    big = ((ROWS, SHARE), BF16)
    def over_b_and_head(value):
        pairs = [(i, i + 1) for i in range(1, count - 1, 2)]
        pairs = pairs + [(j, i) for i, j in pairs]
        crossed = [(2 * i + h, 2 * j + 1 - h) for i, j in pairs for h in range(2)]
        return lax.ppermute(value, ("tm", "head"), crossed)

    xp = over_head(inputs)
    b0 = over_b(inputs)
    b1 = over_b_and_head(inputs)
    *staged, pack = stage(w_query, w_key, w_value, w_out, inputs, cotangent, kernel)
    xp, *staged = lax.optimization_barrier((xp, *staged))
    w_query, w_key, w_value, w_out, inputs, cotangent, kernel = staged
    q, k, v = call(
        own_kernel, (inputs, xp, w_query, w_key, w_value), (big, big, big), us=0.0
    )
    ka = over_a(k)
    va = over_a(v)
    q, pack = lax.optimization_barrier((q, pack))
    pack_p = over_head(pack)
    edge = ((3 * EDGE, D), BF16)
    chunk = [
        (((HEADS, rows, 3 * ROWS), BF16), ((rows, SHARE), BF16), ((rows, D), BF16))
        for rows in (2 * RIM, MID)
    ]
    kb, vb, p_rim, att_rim, rim = call(
        attend_rim_kernel,
        (b0, b1, w_key, w_value, w_out, q, k, v, ka, va),
        (big, big, *chunk[0]),
        us=2.0,
    )
    rim_p = over_head(rim)
    p_mid, att_mid, mid = call(
        attend_mid_kernel, (w_out, q, k, v, ka, va, kb, vb), chunk[1], us=2.0
    )
    mid_p = over_head(mid)
    attended = (att_rim, att_mid, p_rim, p_mid)
    to_a, to_b = call(
        merge_kernel, (rim, rim_p, cotangent, pack_p, inputs, xp), (edge, edge), us=3.0
    )
    chunked_rows = ((CHUNKS, ROWS, LANES), F32)
    wide = ((ROWS, SHARE), F32)
    tall = ((ROWS, LANES), F32)
    n1o, n1p, rstd, cot_chunks = call(
        prepare_kernel, (inputs, xp, cotangent, pack_p), (wide, wide, tall, chunked_rows), us=3.0
    )
    eb = over_b(to_b)
    ea = over_a(to_a)
    chunked = ((CHUNKS, EXT, LANES), F32)
    tall = ((ROWS, LANES), F32)
    output, dh, datt, gk = call(
        conv_kernel,
        (
            inputs, xp, rim, rim_p, mid, mid_p, ea, eb, cot_chunks, pack_p,
            kernel, w_out,
        ),
        (big, ((ROWS, SHARE), F32), big, ((KW, SHARE), F32)),
        scratch=(
            chunked, ((CHUNKS, 2 * EDGE, LANES), F32), chunked, chunked_rows, ((ROWS, SHARE), F32),
            ((CHUNKS, 16, LANES), F32), tall, tall, tall, ((ROWS, D), BF16),
        ),
        us=5.0,
        mib=12,
    )
    assert count == 128
    tap_sums = ((KW, SHARE), F32)

    def swaps(value, steps):
        return [
            lax.ppermute(value, "tm", [(i, i ^ step) for i in range(count)]) for step in steps
        ]

    chain = [gk]
    for steps in ((1,), (32, 64, 96), (8, 16, 24)):
        parts = (chain[-1], *swaps(chain[-1], steps))
        chain.extend(call(sum_kernel, parts, (tap_sums,), us=0.6, mib=1))
    pair = ((2, ROWS, SHARE), BF16)
    dq_b, dkv_b = call(
        functools.partial(back_halo_kernel, which=2),
        (q, kb, vb, datt, *attended),
        (((ROWS, SHARE), F32), pair),
        us=1.5,
    )
    got_b = over_b(dkv_b)
    dq_ab, dkv_a = call(
        functools.partial(back_halo_kernel, which=1),
        (q, ka, va, datt, *attended, dq_b, chain[1]),
        (((ROWS, SHARE), F32), pair),
        us=1.5,
    )
    got_a = over_a(dkv_a)
    dkv, pin = call(
        back_own_kernel,
        (q, k, v, datt, *attended, dq_ab, w_query, chain[1]),
        (((2, ROWS, SHARE), F32), ((ROWS, D), F32)),
        us=2.0,
    )
    send, keep, stat = call(
        project_kernel,
        (n1o, n1p, dkv, got_a, got_b, pin, w_key, w_value, chain[2]),
        (((ROWS, SHARE + LANES), BF16), ((ROWS, SHARE), F32), tall),
        us=1.5,
    )
    got = over_head(send)
    grad, grad_taps = call(
        final_kernel,
        (n1o, rstd, keep, stat, got, dh, chain[3], *swaps(chain[3], (2, 4, 6))),
        (big, tap_sums),
        us=1.0,
    )
    return output, grad, grad_taps


def solution(mesh):
    placed = (
        P("tm", "head"),
        P(None, "head"),
        P(None, "head"),
        P(None, "head"),
        P("head", None),
        P(None, "head"),
        P("tm", "head"),
    )
    return jax.shard_map(
        local,
        mesh=mesh,
        in_specs=placed,
        out_specs=(P("tm", "head"), P("tm", "head"), P(None, "head")),
        check_vma=False,
    )
```

```python
import functools
import jax
import jax.numpy as jnp
from jax import lax
from jax.experimental import pallas as pl
from jax.experimental.pallas import tpu as pltpu
from jax.sharding import PartitionSpec as P

D = 1024
HEAD_DIM = 128
BLOCK = 128
CONTEXT = 2
KW = 9
EPSILON = 1e-05
MASKED = -1e30

ROWS = CONTEXT * BLOCK
SHARE = 512
HEADS = SHARE // HEAD_DIM
LANES = 128
EDGE = 16
RIM = 32
MID = ROWS - 2 * RIM
CHUNKS = D // LANES
HALF_CHUNKS = SHARE // LANES
PAD = 16
EXT = ROWS + 2 * PAD
HALF = KW // 2
SCALE = HEAD_DIM ** (-0.5)
F32 = jnp.float32
BF16 = jnp.bfloat16


def nn(a, b):
    return lax.dot_general(a, b, (((1,), (0,)), ((), ())), preferred_element_type=F32)


def nt(a, b):
    return lax.dot_general(a, b, (((1,), (1,)), ((), ())), preferred_element_type=F32)


def tn(a, b):
    return lax.dot_general(a, b, (((0,), (0,)), ((), ())), preferred_element_type=F32)


def row_sum(a):
    return jnp.sum(a, axis=1, keepdims=True)


def moments(a, b):
    center = (row_sum(a) + row_sum(b)) * (1.0 / D)
    spread = (row_sum(a * a) + row_sum(b * b)) * (1.0 / D) - center * center
    return center, lax.rsqrt(spread + EPSILON)


def norm_pair(a, b):
    a = a.astype(F32)
    b = b.astype(F32)
    center, rstd = moments(a, b)
    return (a - center) * rstd, (b - center) * rstd, rstd


def placement():
    place = lax.axis_index("tm")
    last = lax.axis_size("tm") - 1
    odd = lax.rem(place, 2)
    left = (place > 0).astype(jnp.int32)
    right = (place < last).astype(jnp.int32)
    return odd, left, right


def own_other():
    h = lax.axis_index("head")
    own = pl.ds(pl.multiple_of(h * SHARE, SHARE), SHARE)
    other = pl.ds(pl.multiple_of((1 - h) * SHARE, SHARE), SHARE)
    return own, other


def lanes_of(head):
    return slice(head * HEAD_DIM, (head + 1) * HEAD_DIM)


def band_bias(right, valid, rows):
    row = (lax.broadcasted_iota(jnp.int32, (rows, ROWS), 0) >= rows // 2).astype(jnp.int32)
    col = (lax.broadcasted_iota(jnp.int32, (rows, ROWS), 1) >= BLOCK).astype(jnp.int32)
    hidden = ((row - col) == 1 - 2 * right) | (valid == 0)
    return jnp.where(hidden, MASKED, 0.0).astype(F32)


def own_kernel(xo, xp, wq, wk, wv, q, k, v):
    own, other = own_other()
    no, np_, _ = norm_pair(xo[...], xp[...])
    no = no.astype(BF16)
    np_ = np_.astype(BF16)
    for w, out in ((wq, q), (wk, k), (wv, v)):
        out[...] = (nn(no, w[own, :]) + nn(np_, w[other, :])).astype(BF16)


def halo_kv(xo, xp, wk, wv, k, v):
    own, other = own_other()
    no, np_, _ = norm_pair(xo[...], xp[...])
    no = no.astype(BF16)
    np_ = np_.astype(BF16)
    for w, out in ((wk, k), (wv, v)):
        out[...] = (nn(no, w[own, :]) + nn(np_, w[other, :])).astype(BF16)


def attend(rows, q, k, v, ka, va, kb, vb, wo, p, att, part):
    odd, left, right = placement()
    height = att.shape[0]
    bias_a = band_bias(1 - odd, 1, height)
    bias_b = band_bias(odd, jnp.where(odd == 1, right, left), height)
    for head in range(HEADS):
        f = lanes_of(head)
        qh = jnp.concatenate([q[at, f] for at in rows], axis=0)
        scores = (
            nt(qh, k[:, f]) * SCALE,
            nt(qh, ka[:, f]) * SCALE + bias_a,
            nt(qh, kb[:, f]) * SCALE + bias_b,
        )
        top = functools.reduce(jnp.maximum, scores)
        top = jnp.max(top, axis=1, keepdims=True)
        scores = [jnp.exp(s - top) for s in scores]
        inverse = 1.0 / row_sum(sum(scores))
        out = 0.0
        for n, (s, values) in enumerate(zip(scores, (v, va, vb))):
            s = (s * inverse).astype(BF16)
            p[head, :, n * ROWS:(n + 1) * ROWS] = s
            out = out + nn(s, values[:, f])
        att[:, f] = out.astype(BF16)
    own, other = own_other()
    part[:, :SHARE] = nn(att[...], wo[:, own]).astype(BF16)
    part[:, SHARE:] = nn(att[...], wo[:, other]).astype(BF16)


def attend_rim_kernel(b0, b1, wk, wv, wo, q, k, v, ka, va, kb, vb, p, att, part):
    halo_kv(b0, b1, wk, wv, kb, vb)
    rows = (slice(0, RIM), slice(ROWS - RIM, ROWS))
    attend(rows, q, k, v, ka, va, kb, vb, wo, p, att, part)


def attend_mid_kernel(wo, q, k, v, ka, va, kb, vb, p, att, part):
    attend((slice(RIM, ROWS - RIM),), q, k, v, ka, va, kb, vb, wo, p, att, part)


def in_order(rim, mid):
    return jnp.concatenate([rim[:RIM], mid, rim[RIM:]], axis=0)


def edge_rows(rows):
    odd, _, _ = placement()
    last = rows - EDGE
    return (
        pl.ds(pl.multiple_of((1 - odd) * last, EDGE), EDGE),
        pl.ds(pl.multiple_of(odd * last, EDGE), EDGE),
    )


def merge_kernel(part, part_p, co, cp, xo, xp, to_a, to_b):
    for at, at_c, out in zip(edge_rows(2 * RIM), edge_rows(ROWS), (to_a, to_b)):
        mine = part[at, :].astype(F32)
        theirs = part_p[at, :].astype(F32)
        out[:EDGE, :SHARE] = (mine[:, :SHARE] + theirs[:, SHARE:]).astype(BF16)
        out[:EDGE, SHARE:] = (mine[:, SHARE:] + theirs[:, :SHARE]).astype(BF16)
        out[EDGE:2 * EDGE, :SHARE] = co[at_c, :]
        out[EDGE:2 * EDGE, SHARE:] = cp[at_c, :]
        out[2 * EDGE:, :SHARE] = xo[at_c, :]
        out[2 * EDGE:, SHARE:] = xp[at_c, :]


def prepare_kernel(xo, xp, co, cp, no, np_, rstd, cs):
    no[...], np_[...], scale = norm_pair(xo[...], xp[...])
    rstd[...] = jnp.broadcast_to(scale, (ROWS, LANES))
    for c in range(HALF_CHUNKS):
        f = slice(c * LANES, (c + 1) * LANES)
        cs[c] = co[:, f].astype(F32)
        cs[HALF_CHUNKS + c] = cp[:ROWS, f].astype(F32)


def conv_kernel(
    xo, xp, rim, rim_p, mid, mid_p, ea, eb, cs, cp, to, wo,
    output, dh, datt, gk,
    n2s, ends, dzs, dns, hs, taps, rs2, sum0, sum1, dhb,
):
    odd, left, right = placement()
    own, other = own_other()
    is_odd = odd == 1
    step = 32
    tp = unpack_taps(cp)
    for c in range(HALF_CHUNKS):
        f = slice(c * LANES, (c + 1) * LANES)
        taps[c, :KW, :] = to[:, f]
        taps[HALF_CHUNKS + c, :KW, :] = tp[:, f]

    def rows_in(index, carry, part, part_p, shift):
        r = pl.multiple_of(index * step, step)
        source = pl.ds(pl.multiple_of(r - shift, step), step)
        rows = pl.ds(r, step)
        held = pl.ds(pl.multiple_of(PAD + r, PAD), step)
        p = part[source, :].astype(F32)
        pp = part_p[source, :].astype(F32)
        ho = xo[rows, :].astype(F32) + p[:, :SHARE] + pp[:, SHARE:]
        hp = xp[rows, :].astype(F32) + p[:, SHARE:] + pp[:, :SHARE]
        center, rstd = moments(ho, hp)
        hs[rows, :] = ho
        rs2[rows, :] = jnp.broadcast_to(rstd, (step, LANES))
        for c in range(HALF_CHUNKS):
            f = slice(c * LANES, (c + 1) * LANES)
            n2s[c, held, :] = (ho[:, f] - center) * rstd
            n2s[HALF_CHUNKS + c, held, :] = (hp[:, f] - center) * rstd
        return carry

    for first, last, part, part_p, shift in (
        (0, RIM, rim, rim_p, 0),
        (RIM, ROWS - RIM, mid, mid_p, RIM),
        (ROWS - RIM, ROWS, rim, rim_p, MID),
    ):
        body = functools.partial(rows_in, part=part, part_p=part_p, shift=shift)
        lax.fori_loop(first // step, last // step, body, 0, unroll=True)

    pa = ea[:EDGE, :].astype(F32)
    pb = eb[:EDGE, :].astype(F32)
    sides = (
        (is_odd, 0, 0, left),
        (jnp.logical_not(is_odd), PAD + ROWS, EDGE, right),
    )
    for from_a, at, end, valid in sides:
        def pick(one, two):
            return jnp.where(from_a, one.astype(F32), two.astype(F32))

        pe = pick(pa, pb)
        ho = pick(ea[2 * EDGE:, :SHARE], eb[2 * EDGE:, :SHARE]) + pe[:, :SHARE]
        hp = pick(ea[2 * EDGE:, SHARE:], eb[2 * EDGE:, SHARE:]) + pe[:, SHARE:]
        center, rstd = moments(ho, hp)
        ctan = pick(ea[EDGE:2 * EDGE, :SHARE], eb[EDGE:2 * EDGE, :SHARE])
        ctan_p = pick(ea[EDGE:2 * EDGE, SHARE:], eb[EDGE:2 * EDGE, SHARE:])
        inside = valid == 1
        for c in range(HALF_CHUNKS):
            f = slice(c * LANES, (c + 1) * LANES)
            for d, hh, cc in ((c, ho, ctan), (HALF_CHUNKS + c, hp, ctan_p)):
                n2s[d, at:at + EDGE, :] = jnp.where(inside, (hh[:, f] - center) * rstd, 0.0)
                ends[d, end:end + EDGE, :] = jnp.where(inside, cc[:, f], 0.0)

    piece = 136

    def forward(c, carry, mine):
        w = taps[c]
        for r0 in (8, 8 + piece):
            z = w[0:1, :] * n2s[c, r0 - HALF:r0 - HALF + piece, :]
            for tap in range(1, KW):
                at = r0 + tap - HALF
                z = z + w[tap:tap + 1, :] * n2s[c, at:at + piece, :]
            gate = jax.nn.sigmoid(z)
            if r0 < PAD:
                ctan = jnp.concatenate([ends[c, r0:PAD, :], cs[c, :r0 + piece - PAD, :]], axis=0)
            else:
                ctan = jnp.concatenate([cs[c, r0 - PAD:, :], ends[c, EDGE:PAD + 8, :]], axis=0)
            dzs[c, r0:r0 + piece, :] = ctan * gate * (1.0 + z * (1.0 - gate))
            if mine:
                lo = max(r0, PAD)
                hi = min(r0 + piece, PAD + ROWS)
                lane = pl.ds(pl.multiple_of(c * LANES, LANES), LANES)
                mix = (z * gate)[lo - r0:hi - r0, :]
                output[lo - PAD:hi - PAD, lane] = (hs[lo - PAD:hi - PAD, lane] + mix).astype(BF16)
        return carry

    lax.fori_loop(0, HALF_CHUNKS, functools.partial(forward, mine=True), 0, unroll=2)
    lax.fori_loop(HALF_CHUNKS, CHUNKS, functools.partial(forward, mine=False), 0, unroll=2)

    sum0[...] = jnp.zeros_like(sum0)
    sum1[...] = jnp.zeros_like(sum1)

    def backward(c, carry, mine):
        w = taps[c]
        for r0 in (0, ROWS // 2):
            half = slice(r0, r0 + ROWS // 2)
            n2 = n2s[c, PAD + r0:PAD + r0 + ROWS // 2, :]
            g = 0.0
            for tap in range(KW):
                at = PAD + r0 + HALF - tap
                dz = dzs[c, at:at + ROWS // 2, :]
                g = g + w[tap:tap + 1, :] * dz
                if mine:
                    lane = pl.ds(pl.multiple_of(c * LANES, LANES), LANES)
                    part = jnp.sum(dz * n2, axis=0, keepdims=True)
                    gk[tap:tap + 1, lane] = part if r0 == 0 else gk[tap:tap + 1, lane] + part
            dns[c, half, :] = g
            sum0[half, :] = sum0[half, :] + g
            sum1[half, :] = sum1[half, :] + g * n2
        return carry

    lax.fori_loop(0, HALF_CHUNKS, functools.partial(backward, mine=True), 0, unroll=2)
    lax.fori_loop(HALF_CHUNKS, CHUNKS, functools.partial(backward, mine=False), 0, unroll=2)
    sum0[...] = jnp.broadcast_to(row_sum(sum0[...]) * (1.0 / D), (ROWS, LANES))
    sum1[...] = jnp.broadcast_to(row_sum(sum1[...]) * (1.0 / D), (ROWS, LANES))

    def finish(c, carry, mine):
        lane = pl.ds(pl.multiple_of(c * LANES, LANES), LANES)
        value = cs[c] + rs2[...] * (
            dns[c] - sum0[...] - n2s[c, PAD:PAD + ROWS, :] * sum1[...]
        )
        if mine:
            dh[:, lane] = value
        dhb[:, lane] = value.astype(BF16)
        return carry

    lax.fori_loop(0, HALF_CHUNKS, functools.partial(finish, mine=True), 0, unroll=True)
    lax.fori_loop(HALF_CHUNKS, CHUNKS, functools.partial(finish, mine=False), 0, unroll=True)
    datt[...] = (nt(dhb[:, :SHARE], wo[:, own]) + nt(dhb[:, SHARE:], wo[:, other])).astype(BF16)


def pair_grad(qh, kh, vh, gh, p, delta):
    dots = nt(gh, vh)
    ds = (p.astype(F32) * (dots - delta) * SCALE).astype(BF16)
    return nn(ds, kh), tn(ds, qh), tn(p, gh)


def back_halo_kernel(q, k, v, datt, att, att_mid, p, p_mid, *refs, which):
    if which == 1:
        dq, dkv = refs[-2:]
    else:
        dq, dkv, deltas = refs
    at = slice(which * ROWS, (which + 1) * ROWS)
    for head in range(HEADS):
        f = lanes_of(head)
        gh = datt[:, f]
        if which == 1:
            delta = refs[1][head][:, :1]
        else:
            delta = row_sum(gh.astype(F32) * in_order(att[:, f], att_mid[:, f]).astype(F32))
            deltas[head] = jnp.broadcast_to(delta, (ROWS, LANES))
        probs = in_order(p[head, :, at], p_mid[head, :, at])
        d_q, d_k, d_v = pair_grad(q[:, f], k[:, f], v[:, f], gh, probs, delta)
        dq[:, f] = d_q + refs[0][:, f] if which == 1 else d_q
        dkv[0, :, f] = d_k.astype(BF16)
        dkv[1, :, f] = d_v.astype(BF16)


def back_own_kernel(q, k, v, datt, att, att_mid, p, p_mid, dq_ab, deltas, wq, after, dkv, pin):
    dq = []
    for head in range(HEADS):
        f = lanes_of(head)
        gh = datt[:, f]
        delta = deltas[head][:, :1]
        probs = in_order(p[head, :, :ROWS], p_mid[head, :, :ROWS])
        d_q, d_k, d_v = pair_grad(q[:, f], k[:, f], v[:, f], gh, probs, delta)
        dkv[0, :, f] = d_k
        dkv[1, :, f] = d_v
        dq.append((d_q + dq_ab[:, f]).astype(BF16))
    own, other = own_other()
    dq = jnp.concatenate(dq, axis=1)
    pin[:, :SHARE] = nt(dq, wq[own, :])
    pin[:, SHARE:] = nt(dq, wq[other, :])


def project_kernel(n1o, n1p, dkv, got_a, got_b, pin, wk, wv, after, send, keep, stat):
    own, other = own_other()
    dk = (dkv[0] + got_a[0].astype(F32) + got_b[0].astype(F32)).astype(BF16)
    dv = (dkv[1] + got_a[1].astype(F32) + got_b[1].astype(F32)).astype(BF16)
    p_own = pin[:, :SHARE] + nt(dk, wk[own, :]) + nt(dv, wv[own, :])
    p_other = pin[:, SHARE:] + nt(dk, wk[other, :]) + nt(dv, wv[other, :])
    s0 = row_sum(p_own) + row_sum(p_other)
    s1 = row_sum(p_own * n1o[...]) + row_sum(p_other * n1p[...])
    keep[...] = p_own
    send[:, :SHARE] = p_other.astype(BF16)
    lane = lax.broadcasted_iota(jnp.int32, (ROWS, LANES), 1)
    s0_hi = s0.astype(BF16).astype(F32)
    s1_hi = s1.astype(BF16).astype(F32)
    packed = jnp.where(lane == 0, s0_hi, 0.0)
    packed = jnp.where(lane == 1, s0 - s0_hi, packed)
    packed = jnp.where(lane == 2, s1_hi, packed)
    packed = jnp.where(lane == 3, s1 - s1_hi, packed)
    send[:, SHARE:] = packed.astype(BF16)
    stat[...] = jnp.where(lane == 0, s0, jnp.where(lane == 2, s1, 0.0))


def final_kernel(n1o, rstd, keep, stat, got, dh, row, one, two, three, grad, taps):
    taps[...] = (row[...] + one[...]) + (two[...] + three[...])
    dn1 = keep[...] + got[:, :SHARE].astype(F32)
    lane = lax.broadcasted_iota(jnp.int32, (ROWS, LANES), 1)
    sums = stat[...] + got[:, SHARE:].astype(F32)
    s0 = row_sum(jnp.where(lane < 2, sums, 0.0)) * (1.0 / D)
    s1 = row_sum(jnp.where(lane < 2, 0.0, sums)) * (1.0 / D)
    grad[...] = (dh[...] + rstd[:, :1] * (dn1 - s0 - n1o[...] * s1)).astype(BF16)


def sum_kernel(*refs):
    refs[-1][...] = sum(ref[...] for ref in refs[:-1])


def stage_kernel(*refs):
    half = (len(refs) - 2) // 2
    pack, sems = refs[-2:]
    copies = [
        pltpu.make_async_copy(refs[i], refs[half + i], sems.at[i]) for i in range(half)
    ]
    for copy in copies:
        copy.start()
    for copy in copies:
        copy.wait()
    co, taps = refs[2 * half - 2:2 * half]
    pack[:ROWS, :] = co[...]
    rest = taps[...]
    for n in range(3):
        piece = rest.astype(BF16)
        pack[ROWS + n * EDGE:ROWS + n * EDGE + KW, :] = piece
        rest = rest - piece.astype(F32)


def unpack_taps(pack):
    return sum(
        pack[ROWS + n * EDGE:ROWS + n * EDGE + KW, :].astype(F32) for n in (2, 1, 0)
    )


def stage(*arrays):
    outs = [pltpu.VMEM(a.shape, a.dtype) for a in arrays]
    outs.append(pltpu.VMEM((ROWS + 3 * EDGE, SHARE), BF16))
    return pl.pallas_call(
        stage_kernel,
        out_shape=outs,
        in_specs=[pl.BlockSpec(memory_space=pltpu.HBM)] * len(arrays),
        out_specs=[pl.BlockSpec(memory_space=pltpu.VMEM)] * len(outs),
        scratch_shapes=[pltpu.SemaphoreType.DMA((len(arrays),))],
        compiler_params=pltpu.CompilerParams(vmem_limit_bytes=6 * 1024 * 1024),
        cost_estimate=pl.CostEstimate(flops=0, bytes_accessed=64 * 1024 * 1024, transcendentals=0),
    )(*[pltpu.with_memory_space_constraint(a, pltpu.HBM) for a in arrays])


def call(kernel, args, outs, scratch=(), us=1.0, mib=6):
    whole = pl.BlockSpec(memory_space=pltpu.VMEM)
    return pl.pallas_call(
        kernel,
        out_shape=[jax.ShapeDtypeStruct(shape, dtype) for shape, dtype in outs],
        in_specs=[whole] * len(args),
        out_specs=[whole] * len(outs),
        scratch_shapes=[pltpu.VMEM(shape, dtype) for shape, dtype in scratch],
        compiler_params=pltpu.CompilerParams(vmem_limit_bytes=mib * 1024 * 1024),
        cost_estimate=pl.CostEstimate(
            flops=int(us * 1e10), bytes_accessed=int(us * 1e7), transcendentals=0
        ),
    )(*args)


def local(inputs, w_query, w_key, w_value, w_out, kernel, cotangent):
    count = lax.axis_size("tm")
    assert inputs.shape == (ROWS, SHARE) and count % 2 == 0
    def over_head(value):
        return lax.ppermute(value, "head", [(0, 1), (1, 0)])

    def over_a(value):
        return lax.ppermute(value, "tm", [(i, i ^ 1) for i in range(count)])

    def over_b(value):
        pairs = [(i, i + 1) for i in range(1, count - 1, 2)]
        return lax.ppermute(value, "tm", pairs + [(j, i) for i, j in pairs])

    big = ((ROWS, SHARE), BF16)
    def over_b_and_head(value):
        pairs = [(i, i + 1) for i in range(1, count - 1, 2)]
        pairs = pairs + [(j, i) for i, j in pairs]
        crossed = [(2 * i + h, 2 * j + 1 - h) for i, j in pairs for h in range(2)]
        return lax.ppermute(value, ("tm", "head"), crossed)

    xp = over_head(inputs)
    b0 = over_b(inputs)
    b1 = over_b_and_head(inputs)
    *staged, pack = stage(w_query, w_key, w_value, w_out, inputs, cotangent, kernel)
    xp, *staged = lax.optimization_barrier((xp, *staged))
    w_query, w_key, w_value, w_out, inputs, cotangent, kernel = staged
    q, k, v = call(
        own_kernel, (inputs, xp, w_query, w_key, w_value), (big, big, big), us=0.0
    )
    ka = over_a(k)
    va = over_a(v)
    q, pack = lax.optimization_barrier((q, pack))
    pack_p = over_head(pack)
    edge = ((3 * EDGE, D), BF16)
    chunk = [
        (((HEADS, rows, 3 * ROWS), BF16), ((rows, SHARE), BF16), ((rows, D), BF16))
        for rows in (2 * RIM, MID)
    ]
    kb, vb, p_rim, att_rim, rim = call(
        attend_rim_kernel,
        (b0, b1, w_key, w_value, w_out, q, k, v, ka, va),
        (big, big, *chunk[0]),
        us=2.0,
    )
    rim_p = over_head(rim)
    p_mid, att_mid, mid = call(
        attend_mid_kernel, (w_out, q, k, v, ka, va, kb, vb), chunk[1], us=2.0
    )
    mid_p = over_head(mid)
    attended = (att_rim, att_mid, p_rim, p_mid)
    to_a, to_b = call(
        merge_kernel, (rim, rim_p, cotangent, pack_p, inputs, xp), (edge, edge), us=3.0
    )
    chunked_rows = ((CHUNKS, ROWS, LANES), F32)
    wide = ((ROWS, SHARE), F32)
    tall = ((ROWS, LANES), F32)
    n1o, n1p, rstd, cot_chunks = call(
        prepare_kernel, (inputs, xp, cotangent, pack_p), (wide, wide, tall, chunked_rows), us=3.0
    )
    eb = over_b(to_b)
    ea = over_a(to_a)
    chunked = ((CHUNKS, EXT, LANES), F32)
    tall = ((ROWS, LANES), F32)
    output, dh, datt, gk = call(
        conv_kernel,
        (
            inputs, xp, rim, rim_p, mid, mid_p, ea, eb, cot_chunks, pack_p,
            kernel, w_out,
        ),
        (big, ((ROWS, SHARE), F32), big, ((KW, SHARE), F32)),
        scratch=(
            chunked, ((CHUNKS, 2 * EDGE, LANES), F32), chunked, chunked_rows, ((ROWS, SHARE), F32),
            ((CHUNKS, 16, LANES), F32), tall, tall, tall, ((ROWS, D), BF16),
        ),
        us=5.0,
        mib=12,
    )
    assert count == 128
    tap_sums = ((KW, SHARE), F32)

    def swaps(value, steps):
        return [
            lax.ppermute(value, "tm", [(i, i ^ step) for i in range(count)]) for step in steps
        ]

    chain = [gk]
    for steps in ((1,), (32, 96, 64), (8, 16, 24)):
        parts = (chain[-1], *swaps(chain[-1], steps))
        chain.extend(call(sum_kernel, parts, (tap_sums,), us=0.6, mib=1))
    pair = ((2, ROWS, SHARE), BF16)
    dq_b, dkv_b, deltas = call(
        functools.partial(back_halo_kernel, which=2),
        (q, kb, vb, datt, *attended),
        (((ROWS, SHARE), F32), pair, ((HEADS, ROWS, LANES), F32)),
        us=1.5,
    )
    got_b = over_b(dkv_b)
    dq_ab, dkv_a = call(
        functools.partial(back_halo_kernel, which=1),
        (q, ka, va, datt, *attended, dq_b, deltas, chain[1]),
        (((ROWS, SHARE), F32), pair),
        us=1.5,
    )
    got_a = over_a(dkv_a)
    dkv, pin = call(
        back_own_kernel,
        (q, k, v, datt, *attended, dq_ab, deltas, w_query, chain[1]),
        (((2, ROWS, SHARE), F32), ((ROWS, D), F32)),
        us=2.0,
    )
    send, keep, stat = call(
        project_kernel,
        (n1o, n1p, dkv, got_a, got_b, pin, w_key, w_value, chain[2]),
        (((ROWS, SHARE + LANES), BF16), ((ROWS, SHARE), F32), tall),
        us=1.5,
    )
    got = over_head(send)
    grad, grad_taps = call(
        final_kernel,
        (n1o, rstd, keep, stat, got, dh, chain[3], *swaps(chain[3], (2, 6, 4))),
        (big, tap_sums),
        us=1.0,
    )
    return output, grad, grad_taps


def solution(mesh):
    placed = (
        P("tm", "head"),
        P(None, "head"),
        P(None, "head"),
        P(None, "head"),
        P("head", None),
        P(None, "head"),
        P("tm", "head"),
    )
    return jax.shard_map(
        local,
        mesh=mesh,
        in_specs=placed,
        out_specs=(P("tm", "head"), P("tm", "head"), P(None, "head")),
        check_vma=False,
    )
```
